32 devices in a mesh: dom: 2 (over x), frame: 16 (over z, y, core).
Axes of the slice: x: 2, y: 2, z: 4, core: 2. Of those that a mesh axis runs over, the one named last changes fastest.
Arguments:
- queries: bfloat16 [32, 512, 1024], P(('dom', 'frame')), parts along dimension 0, may hold values from -8 to 8
- keys: bfloat16 [32, 512, 1024], P(('dom', 'frame')), parts along dimension 0, may hold values from -8 to 8
- values: bfloat16 [32, 512, 1024], P(('dom', 'frame')), parts along dimension 0, may hold values from -6 to 6
- grad_out: bfloat16 [32, 512, 1024], P(('dom', 'frame')), parts along dimension 0, may hold values from -6 to 6
- links: int32 [32, 4], P(('dom', 'frame')), parts along dimension 0, may hold values from 0 to 1, as said below
- w_query: bfloat16 [1024, 1024], replicated, may hold values from -0.1875 to 0.1875
- w_key: bfloat16 [1024, 1024], replicated, may hold values from -0.1875 to 0.1875
- w_value: bfloat16 [1024, 1024], replicated, may hold values from -0.1875 to 0.1875
Outputs:
- grad_input: bfloat16 [32, 512, 1024], P(('dom', 'frame')), parts along dimension 0
The draws below stay inside these ranges and needn't reach their ends.
There are 2 independent parts, one for each index of `dom`. The reference program is written for one: setup_inputs(seed, part) draws one part's arguments, and reference() takes and returns one part's arrays. A program takes and returns all parts, laid end to end along the dimension named above; an argument that names none is the same for every part. Nothing has to cross between parts.
Inputs may be any that keep to these rules, and one draw needn't show every extreme that they name: links[t, j] is 0 whenever t < 2**j; otherwise 0 or 1, so frames attend to ragged numbers of up to 4 earlier frames.
All inputs are finite; a program needn't handle non-finite values.
Results may differ from the reference program's by a relative error of at most 0.0049.
Values may be sent and summed in bfloat16 or wider, within the bound.
No kernel may reach another device: no remote copies, remote signals or barrier semaphores. Data moves between devices by JAX's collectives and lax.ppermute only.
A program may use at most 128 MiB of HBM per device.

```python
import jax
import jax.numpy as jnp
from jax import lax

D = 1024
HEADS = 16
PATCH = 512
NDIL = 4
FRAMES = 16


def base_draw(key, salt_value):
    sub_key = jax.random.fold_in(key, salt_value)
    return jnp.clip(jax.random.normal(sub_key, (FRAMES, PATCH, D), jnp.float32), -6.0, 6.0)


def draw_queries(key, part):
    base_field = base_draw(key, 1)
    return base_field.astype(jnp.bfloat16)


def draw_keys(key, part):
    base_field = base_draw(key, 2)
    return base_field.astype(jnp.bfloat16)


def draw_links(key, part):
    link_bits = jax.random.randint(jax.random.fold_in(key, 3), (FRAMES, NDIL), 0, 4)
    frame_ids = lax.broadcasted_iota(jnp.int32, (FRAMES, NDIL), 0)
    columns = lax.broadcasted_iota(jnp.int32, (FRAMES, NDIL), 1)
    spacings = jnp.left_shift(jnp.ones((FRAMES, NDIL), jnp.int32), columns)
    return jnp.where((link_bits > 0) & (frame_ids >= spacings), 1, 0).astype(jnp.int32)


def shard_levels(stream_key, dims, cuts, least, largest):
    loudness = 1.0
    for position, blocks in cuts:
        steps = jax.random.uniform(jax.random.fold_in(jax.random.fold_in(stream_key, 6), position), (blocks,), jnp.float32, least / len(cuts), largest / len(cuts))
        loudness = loudness * jnp.repeat(jnp.exp(steps), dims[position] // blocks).reshape((-1,) + (1,) * (len(dims) - 1 - position))
    return loudness


def gaussian(own_key, extent, width, bound, shards=(), dtype=jnp.bfloat16):
    level = shard_levels(own_key, extent, shards, -0.22, 0.18) if shards else 1.0
    result = jax.random.normal(own_key, extent, jnp.float32) * width * level
    return jnp.minimum(jnp.maximum(result, -bound), bound).astype(dtype)


def setup_inputs(seed: int = 0, part: int = 0) -> dict:
    arg_keys = jax.random.split(jax.random.key(seed), 9)
    part_keys = jax.random.split(jax.random.fold_in(arg_keys[8], part), 9)
    return {
        "queries": draw_queries(jax.random.fold_in(jax.random.fold_in(arg_keys[8], part), 71), part),
        "keys": draw_keys(jax.random.fold_in(jax.random.fold_in(arg_keys[8], part), 71), part),
        "values": gaussian(part_keys[2], (FRAMES, PATCH, D), 1.0, 6.0, ((0, 16),)),
        "grad_out": gaussian(part_keys[3], (FRAMES, PATCH, D), 1.0, 6.0, ((0, 16),)),
        "links": draw_links(jax.random.fold_in(jax.random.fold_in(arg_keys[8], part), 71), part),
        "w_query": gaussian(arg_keys[5], (D, D), D ** -0.5, 0.1875),
        "w_key": gaussian(arg_keys[6], (D, D), D ** -0.5, 0.1875),
        "w_value": gaussian(arg_keys[7], (D, D), D ** -0.5, 0.1875),
    }


def attention_core(query_f, grad_f, key_list, value_list, live_list, score_scale):
    live_mask = jnp.stack([m[:, None, None] for m in live_list])
    scores = jnp.stack([jnp.sum(query_f * k, axis=-1) for k in key_list]) * score_scale
    scores = jnp.where(live_mask > 0, scores, -1e30)
    highest = jnp.max(scores, axis=0)
    weights_raw = jnp.exp(scores - highest) * live_mask
    probability = weights_raw / jnp.sum(weights_raw, axis=0)
    grad_prob = jnp.stack([jnp.sum(grad_f * v, axis=-1) for v in value_list])
    inner_sum = jnp.sum(probability * grad_prob, axis=0)
    grad_score = probability * (grad_prob - inner_sum) * score_scale
    grad_query = jnp.zeros_like(query_f)
    grad_keys = []
    grad_values = []
    for i in range(len(key_list)):
        grad_query = grad_query + grad_score[i][..., None] * key_list[i]
        grad_keys.append(grad_score[i][..., None] * query_f)
        grad_values.append(probability[i][..., None] * grad_f)
    return grad_query, grad_keys, grad_values


def dot_transposed(left, weight):
    return lax.dot_general(left, weight, (((1,), (1,)), ((), ())), preferred_element_type=jnp.float32)


def reference(queries, keys, values, grad_out, links, w_query, w_key, w_value):
    frames, patches, model_width = queries.shape
    head_size = model_width // HEADS
    score_scale = head_size ** -0.5
    block_rows = 64 if patches % 64 == 0 else patches
    block_count = patches // block_rows

    def split_blocks(a):
        return a.reshape(frames, block_count, block_rows, model_width).transpose(1, 0, 2, 3)

    def spread_heads(a):
        return a.astype(jnp.float32).reshape(frames, block_rows, HEADS, head_size)

    def per_block(pieces):
        query_b, key_b, value_b, grad_b = pieces
        query_f = spread_heads(query_b)
        grad_f = spread_heads(grad_b)
        key_f = spread_heads(key_b)
        value_f = spread_heads(value_b)
        key_list = [key_f]
        value_list = [value_f]
        live_list = [jnp.ones((frames,), jnp.float32)]
        for j in range(NDIL):
            spacing = 2 ** j
            padding = jnp.zeros((spacing, block_rows, HEADS, head_size), jnp.float32)
            key_list.append(jnp.concatenate([padding, key_f[:frames - spacing]], axis=0))
            value_list.append(jnp.concatenate([padding, value_f[:frames - spacing]], axis=0))
            live_list.append((links[:, j] > 0).astype(jnp.float32))
        grad_query, grad_keys, grad_values = attention_core(query_f, grad_f, key_list, value_list, live_list, score_scale)
        key_total = grad_keys[0]
        value_total = grad_values[0]
        for j in range(NDIL):
            spacing = 2 ** j
            padding = jnp.zeros((spacing, block_rows, HEADS, head_size), jnp.float32)
            key_total = key_total + jnp.concatenate([grad_keys[j + 1][spacing:], padding], axis=0)
            value_total = value_total + jnp.concatenate([grad_values[j + 1][spacing:], padding], axis=0)
        shape_out = (frames, block_rows, model_width)
        return (grad_query.reshape(shape_out).astype(jnp.bfloat16),
                key_total.reshape(shape_out).astype(jnp.bfloat16),
                value_total.reshape(shape_out).astype(jnp.bfloat16))

    grad_query, grad_key, grad_value = lax.map(
        per_block, (split_blocks(queries), split_blocks(keys), split_blocks(values), split_blocks(grad_out)))

    def join_blocks(a):
        return a.transpose(1, 0, 2, 3).reshape(frames * patches, model_width)

    total = dot_transposed(join_blocks(grad_query), w_query)
    total = total + dot_transposed(join_blocks(grad_key), w_key)
    total = total + dot_transposed(join_blocks(grad_value), w_value)
    return total.reshape(frames, patches, model_width).astype(jnp.bfloat16)
```

```python
import functools

import jax
import jax.numpy as jnp
from jax import lax
from jax.experimental import pallas as pl
from jax.experimental.pallas import tpu as pltpu
from jax.sharding import PartitionSpec as P

HEADS = 16
NDIL = 4
LANES = 128
VMEM_BYTES = 56 * 2**20
CHUNKS = (2, 2)


def shift(block, distance):
    n = lax.axis_size("frame")
    return lax.ppermute(block, "frame", [(i, i + distance) for i in range(n) if 0 <= i + distance < n])


def swap(block, bit):
    n = lax.axis_size("frame")
    return lax.ppermute(block, "frame", [(i, i ^ bit) for i in range(n)])


def head_rows(width, head_size):
    row = lax.broadcasted_iota(jnp.int32, (HEADS, width), 0)
    feature = lax.broadcasted_iota(jnp.int32, (HEADS, width), 1)
    return jnp.where(feature // head_size == row, 1.0, 0.0).astype(jnp.bfloat16)


def spread_matrix(slot, width, head_size):
    row = lax.broadcasted_iota(jnp.int32, (2 * LANES, width), 0) % LANES
    feature = lax.broadcasted_iota(jnp.int32, (2 * LANES, width), 1)
    return jnp.where(feature // head_size + slot * HEADS == row, 1.0, 0.0).astype(jnp.bfloat16)


def split_high_low(wide):
    high = wide.astype(jnp.bfloat16)
    return high, (wide - high.astype(jnp.float32)).astype(jnp.bfloat16)


def dot(left, right, left_dim, right_dim):
    return lax.dot_general(
        left, right, (((left_dim,), (right_dim,)), ((), ())), preferred_element_type=jnp.float32
    )


def spread_operand(per_source):
    rows = per_source[0].shape[1]
    gap = LANES - HEADS * len(per_source)
    stacked = jnp.concatenate([*per_source, jnp.zeros((gap, rows), jnp.float32)], axis=0)
    return jnp.concatenate(split_high_low(stacked.T), axis=1)


def score_kernel(head_size, flags, query_grad, own, first, second, near, far8, far4, spread, rows_ref,
                 pair1, pair2, pair4, pair8, self_pair, grad_query):
    scale = head_size ** (-0.5)
    width = query_grad.shape[2]
    heads = rows_ref[...]
    query = query_grad[0].astype(jnp.float32)
    grad = query_grad[1].astype(jnp.float32)
    two_first = flags[NDIL] > 0
    one_first = flags[NDIL + 1] > 0

    def pick(use_first, a, b, i):
        return jnp.where(use_first, a[i], b[i])

    getters = (
        lambda i: own[i],
        lambda i: pick(one_first, near[0], near[1], i),
        lambda i: pick(two_first, first, second, i),
        lambda i: far4[i],
        lambda i: far8[i],
    )

    def per_head(left, right):
        high, low = split_high_low(left * right.astype(jnp.float32))
        return dot(heads, high, 1, 1) + dot(heads, low, 1, 1)

    scores, grad_probs = [], []
    for slot, get in enumerate(getters):
        score = per_head(query, get(0)) * scale
        if slot:
            score = jnp.where(flags[slot - 1] > 0, score, -1e30)
        scores.append(score)
        grad_probs.append(per_head(grad, get(1)))
    highest = functools.reduce(jnp.maximum, scores)
    raw = [jnp.exp(s - highest) for s in scores]
    raw = raw[:1] + [jnp.where(flags[j] > 0, r, 0.0) for j, r in enumerate(raw[1:])]
    total = functools.reduce(jnp.add, raw)
    probability = [r / total for r in raw]
    inner = functools.reduce(jnp.add, [p * g for p, g in zip(probability, grad_probs)])
    grad_score = [p * (g - inner) * scale for p, g in zip(probability, grad_probs)]
    for slot, out in enumerate((self_pair, pair1, pair2, pair4, pair8)):
        out[:HEADS, :] = grad_score[slot]
        out[HEADS:, :] = probability[slot]
    operand = spread_operand(grad_score)
    sum_ = None
    for slot, get in enumerate(getters):
        term = dot(operand, spread[slot], 1, 0) * get(0).astype(jnp.float32)
        sum_ = term if sum_ is None else sum_ + term
    grad_query[...] = sum_.astype(jnp.bfloat16)


def sum_kernel(flags, own, first, second, near, far8, far4, self_pair, pair1, pair2, pair4, pair8,
               grad_query, spread, w_query, w_key, w_value, out):
    two_first = flags[NDIL] == 0
    one_first = flags[NDIL + 1] == 0

    def pick(use_first, a, b, i):
        return jnp.where(use_first, a[i], b[i])

    getters = (
        lambda i: own[i],
        lambda i: pick(one_first, near[0], near[1], i),
        lambda i: pick(two_first, first, second, i),
        lambda i: far4[i],
        lambda i: far8[i],
    )
    pairs = (self_pair, pair1, pair2, pair4, pair8)
    sums = []
    for part in range(2):
        operand = spread_operand([p[part * HEADS:(part + 1) * HEADS, :] for p in pairs])
        sum_ = None
        for slot, get in enumerate(getters):
            term = dot(operand, spread[slot], 1, 0) * get(part).astype(jnp.float32)
            sum_ = term if sum_ is None else sum_ + term
        sums.append(sum_.astype(jnp.bfloat16))
    total = dot(grad_query[...], w_query[...], 1, 1)
    total = total + dot(sums[0], w_key[...], 1, 1)
    total = total + dot(sums[1], w_value[...], 1, 1)
    out[...] = total.astype(jnp.bfloat16)


def whole(a):
    return pl.BlockSpec(a.shape, lambda i: (0,) * a.ndim)


def by_rows(width, tile):
    return pl.BlockSpec((2, tile, width), lambda i: (0, i, 0))


def params():
    return pltpu.CompilerParams(vmem_limit_bytes=VMEM_BYTES, dimension_semantics=("arbitrary",))


def scores_of(flags, query_grad, own, first, second, near, far8, far4, spread, rows_of_heads, head_size, tile):
    _, rows, width = own.shape
    wide = by_rows(width, tile)
    pair = pl.BlockSpec((2 * HEADS, tile), lambda i: (0, i))
    pair_shape = jax.ShapeDtypeStruct((2 * HEADS, rows), jnp.float32)

    def kernel(flags_ref, qg, kv, a, b, c, d, e, f, sp, rw, *outs):
        score_kernel(head_size, flags_ref, qg, kv, a, b, (c, d), e, f, sp, rw, *outs)

    return pl.pallas_call(
        kernel,
        grid=(rows // tile,),
        in_specs=[pl.BlockSpec(memory_space=pltpu.SMEM)] + [wide] * 8 + [whole(spread), whole(rows_of_heads)],
        out_specs=[pair] * 5 + [pl.BlockSpec((tile, width), lambda i: (i, 0))],
        out_shape=[pair_shape] * 5 + [jax.ShapeDtypeStruct((rows, width), jnp.bfloat16)],
        compiler_params=params(),
        cost_estimate=pl.CostEstimate(flops=rows * width * 4000, bytes_accessed=rows * width * 36, transcendentals=0),
        name="scores",
    )(flags, query_grad, own, first, second, *near, far8, far4, spread, rows_of_heads)


def sums_of(flags, own, first, second, near, far8, far4, pairs, grad_query, spread, weights, tile):
    _, rows, width = own.shape
    wide = by_rows(width, tile)
    pair = pl.BlockSpec((2 * HEADS, tile), lambda i: (0, i))

    def kernel(flags_ref, qg, a, b, c, d, e, f, p0, p1, p2, p4, p8, gq, sp, wq, wk, wv, out):
        sum_kernel(flags_ref, qg, a, b, (c, d), e, f, p0, p1, p2, p4, p8, gq, sp, wq, wk, wv, out)

    return pl.pallas_call(
        kernel,
        grid=(rows // tile,),
        in_specs=[pl.BlockSpec(memory_space=pltpu.SMEM)] + [wide] * 7 + [pair] * 5
        + [pl.BlockSpec((tile, width), lambda i: (i, 0)), whole(spread)] + [whole(w) for w in weights],
        out_specs=pl.BlockSpec((tile, width), lambda i: (i, 0)),
        out_shape=jax.ShapeDtypeStruct((rows, width), jnp.bfloat16),
        compiler_params=params(),
        cost_estimate=pl.CostEstimate(flops=rows * width * 8000, bytes_accessed=rows * width * 36, transcendentals=0),
        name="sums",
    )(flags, own, first, second, *near, far8, far4, *pairs, grad_query, spread, *weights)


def per_device(queries, keys, values, grad_out, links, w_query, w_key, w_value):
    _, patches, width = queries.shape
    head_size = width // HEADS
    me = lax.axis_index("frame")
    bit0 = lax.rem(me, 2)
    bit1 = lax.rem(me // 2, 2)
    flags = jnp.concatenate([links[0].astype(jnp.int32), jnp.stack([bit1, bit0]).astype(jnp.int32)])
    spread = jnp.stack([spread_matrix(s, width, head_size) for s in range(NDIL + 1)])
    rows_of_heads = head_rows(width, head_size)

    tile = LANES
    unit = patches // sum(CHUNKS)
    bounds = [0]
    for c in CHUNKS:
        bounds.append(bounds[-1] + c * unit)
    chunks = list(zip(bounds[:-1], bounds[1:]))

    key_value, query_grad = [], []
    for lo, hi in chunks:
        key_value.append(jnp.stack([keys[0, lo:hi], values[0, lo:hi]]))
        query_grad.append(jnp.stack([queries[0, lo:hi], grad_out[0, lo:hi]]))
    up4, down4, up8, down8, y_own, y_far, c_own, c_far = [], [], [], [], [], [], [], []
    for kv, qg in zip(key_value, query_grad):
        up4.append(shift(kv, 4))
        down4.append(shift(qg, -4))
        y_own.append(swap(jnp.where(bit1 == 0, kv, qg), 2))
        c_own.append(swap(jnp.where(bit0 == 0, kv, qg), 1))
    for i in range(len(chunks)):
        up8.append(shift(up4[i], 4))
        down8.append(shift(down4[i], -4))
        y_far.append(swap(jnp.where(bit1 == 0, down4[i], up4[i]), 2))
    for i in range(len(chunks)):
        c_far.append(swap(jnp.where(bit0 == bit1, y_own[i], y_far[i]), 1))
    outs = []
    for i in range(len(chunks)):
        near = (c_own[i], c_far[i])
        pair1, pair2, pair4, pair8, self_pair, grad_query = scores_of(
            flags, query_grad[i], key_value[i], y_own[i], y_far[i], near, up8[i], up4[i], spread, rows_of_heads,
            head_size, tile)
        came = [shift(p, -d) for p, d in ((pair1, 1), (pair2, 2), (pair4, 4), (pair8, 8))]
        outs.append(sums_of(flags, query_grad[i], y_own[i], y_far[i], near, down8[i], down4[i], [self_pair, *came],
                            grad_query, spread, (w_query, w_key, w_value), tile))
    return jnp.concatenate(outs, axis=0)[None]


def solution(mesh):
    by_frame = P(("dom", "frame"), None, None)
    return jax.shard_map(
        per_device,
        mesh=mesh,
        in_specs=(by_frame,) * 4 + (P(("dom", "frame"), None), P(), P(), P()),
        out_specs=by_frame,
        check_vma=False,
    )
```

```python
import functools

import jax
import jax.numpy as jnp
from jax import lax
from jax.experimental import pallas as pl
from jax.experimental.pallas import tpu as pltpu
from jax.sharding import PartitionSpec as P

HEADS = 16
NDIL = 4
LANES = 128
VMEM_BYTES = 40 * 2**20
CHUNKS = (2, 2)


def shift(block, distance):
    n = lax.axis_size("frame")
    return lax.ppermute(block, "frame", [(i, i + distance) for i in range(n) if 0 <= i + distance < n])


def swap(block, bit):
    n = lax.axis_size("frame")
    return lax.ppermute(block, "frame", [(i, i ^ bit) for i in range(n)])


def params():
    return pltpu.CompilerParams(vmem_limit_bytes=VMEM_BYTES, dimension_semantics=("arbitrary",))


SMEM = pl.BlockSpec(memory_space=pltpu.SMEM)


def columns(width, tile, offset=0):
    return pl.BlockSpec((2, width, tile), lambda i: (0, 0, i + offset))


def pack(flags, queries, keys, values, grad_out, bounds):
    _, patches, width = queries.shape
    n_chunks = len(bounds) - 1
    tile = LANES

    def kernel(flags_ref, q_ref, k_ref, v_ref, g_ref, *outs):
        kv_outs, qg_outs = outs[:n_chunks], outs[n_chunks:2 * n_chunks]
        y_out, c_out = outs[2 * n_chunks:]
        step = pl.program_id(0)
        kv = [r[0].T for r in (k_ref, v_ref)]
        qg = [r[0].T for r in (q_ref, g_ref)]
        for c in range(n_chunks):
            @pl.when((step >= bounds[c] // tile) & (step < bounds[c + 1] // tile))
            def _(c=c):
                for part in range(2):
                    kv_outs[c][part] = kv[part]
                    qg_outs[c][part] = qg[part]
        for out, flag in ((y_out, NDIL), (c_out, NDIL + 1)):
            @pl.when(flags_ref[flag] == 0)
            def _(out=out):
                for part in range(2):
                    out[part] = kv[part]

            @pl.when(flags_ref[flag] != 0)
            def _(out=out):
                for part in range(2):
                    out[part] = qg[part]

    def chunk_spec(c):
        lo, hi = bounds[c] // tile, bounds[c + 1] // tile
        return pl.BlockSpec((2, width, tile), lambda i: (0, 0, jnp.clip(i - lo, 0, hi - lo - 1)))

    chunk_shapes = [jax.ShapeDtypeStruct((2, width, hi - lo), jnp.bfloat16) for lo, hi in zip(bounds[:-1], bounds[1:])]
    whole_shape = jax.ShapeDtypeStruct((2, width, patches), jnp.bfloat16)
    outs = pl.pallas_call(
        kernel,
        grid=(patches // tile,),
        in_specs=[SMEM] + [pl.BlockSpec((1, tile, width), lambda i: (0, i, 0))] * 4,
        out_specs=[chunk_spec(c) for c in range(n_chunks)] * 2 + [columns(width, tile)] * 2,
        out_shape=chunk_shapes * 2 + [whole_shape] * 2,
        compiler_params=params(),
        name="pack",
    )(flags, queries, keys, values, grad_out)
    return outs[:n_chunks], outs[n_chunks:2 * n_chunks], outs[-2], outs[-1]


def source_getters(own, first, second, near, far4, far8, two_first, one_first):
    return (
        lambda i, rows: own[i, rows, :],
        lambda i, rows: jnp.where(one_first, near[0][i, rows, :], near[1][i, rows, :]),
        lambda i, rows: jnp.where(two_first, first[i, rows, :], second[i, rows, :]),
        lambda i, rows: far4[i, rows, :],
        lambda i, rows: far8[i, rows, :],
    )


def score_kernel(head_size, flags, qg, own, first, second, near_a, near_b, far4, far8, self_pair, pair1, pair2, pair4,
                 pair8, grad_query, score_ref, prob_ref):
    scale = head_size ** (-0.5)
    getters = source_getters(own, first, second, (near_a, near_b), far4, far8, flags[NDIL] > 0, flags[NDIL + 1] > 0)
    for h in range(HEADS):
        rows = slice(h * head_size, (h + 1) * head_size)
        for part, into in ((0, score_ref), (1, prob_ref)):
            mine = qg[part, rows, :].astype(jnp.float32)
            for slot, get in enumerate(getters):
                other = get(part, rows).astype(jnp.float32)
                into[slot, h:h + 1, :] = jnp.sum(mine * other, axis=0, keepdims=True)
    scores = [score_ref[slot] * scale for slot in range(NDIL + 1)]
    scores = scores[:1] + [jnp.where(flags[j] > 0, s, -1e30) for j, s in enumerate(scores[1:])]
    highest = functools.reduce(jnp.maximum, scores)
    raw = [jnp.exp(s - highest) for s in scores]
    raw = raw[:1] + [jnp.where(flags[j] > 0, r, 0.0) for j, r in enumerate(raw[1:])]
    total = functools.reduce(jnp.add, raw)
    probability = [r / total for r in raw]
    grad_probs = [prob_ref[slot] for slot in range(NDIL + 1)]
    inner = functools.reduce(jnp.add, [p * g for p, g in zip(probability, grad_probs)])
    pairs = (self_pair, pair1, pair2, pair4, pair8)
    for slot, (p, g) in enumerate(zip(probability, grad_probs)):
        pairs[slot][:HEADS, :] = p * (g - inner) * scale
        pairs[slot][HEADS:, :] = p
    for h in range(HEADS):
        rows = slice(h * head_size, (h + 1) * head_size)
        terms = [pairs[s][h:h + 1, :] * get(0, rows).astype(jnp.float32) for s, get in enumerate(getters)]
        grad_query[rows, :] = functools.reduce(jnp.add, terms).astype(jnp.bfloat16)


def scores_of(flags, qg, own, first, second, near_a, near_b, far4, far8, start, head_size):
    _, width, rows = own.shape
    tile = LANES
    chunk, whole = columns(width, tile), columns(width, tile, start // tile)
    pair = pl.BlockSpec((2 * HEADS, tile), lambda i: (0, i))
    pair_shape = jax.ShapeDtypeStruct((2 * HEADS, rows), jnp.float32)
    return pl.pallas_call(
        functools.partial(score_kernel, head_size),
        grid=(rows // tile,),
        in_specs=[SMEM, chunk, chunk, whole, chunk, whole, chunk, chunk, chunk],
        out_specs=[pair] * 5 + [pl.BlockSpec((width, tile), lambda i: (0, i))],
        out_shape=[pair_shape] * 5 + [jax.ShapeDtypeStruct((width, rows), jnp.bfloat16)],
        scratch_shapes=[pltpu.VMEM((NDIL + 1, HEADS, tile), jnp.float32)] * 2,
        compiler_params=params(),
        cost_estimate=pl.CostEstimate(flops=rows * width * 100, bytes_accessed=rows * width * 36, transcendentals=0),
        name="scores",
    )(flags, qg, own, first, second, near_a, near_b, far4, far8)


def sum_kernel(head_size, flags, own, first, second, near_a, near_b, far4, far8, self_pair, pair1, pair2, pair4, pair8,
               grad_query, w_query, w_key, w_value, *rest):
    out, key_ref, value_ref, wq, wk, wv, sems = rest[-7:]
    copies = [pltpu.make_async_copy(a, b, sems.at[i])
              for i, (a, b) in enumerate(((w_query, wq), (w_key, wk), (w_value, wv)))]

    @pl.when(pl.program_id(0) == 0)
    def _():
        for copy in copies:
            copy.start()

    getters = source_getters(own, first, second, (near_a, near_b), far4, far8, flags[NDIL] == 0, flags[NDIL + 1] == 0)
    pairs = (self_pair, pair1, pair2, pair4, pair8)
    for h in range(HEADS):
        rows = slice(h * head_size, (h + 1) * head_size)
        for part, into in ((0, key_ref), (1, value_ref)):
            row = part * HEADS + h
            terms = [pairs[s][row:row + 1, :] * get(part, rows).astype(jnp.float32) for s, get in enumerate(getters)]
            into[rows, :] = functools.reduce(jnp.add, terms).astype(jnp.bfloat16)

    @pl.when(pl.program_id(0) == 0)
    def _():
        for copy in copies:
            copy.wait()

    total = jnp.dot(wq[...], grad_query[...], preferred_element_type=jnp.float32)
    total = total + jnp.dot(wk[...], key_ref[...], preferred_element_type=jnp.float32)
    total = total + jnp.dot(wv[...], value_ref[...], preferred_element_type=jnp.float32)
    out[...] = total.T.astype(jnp.bfloat16)


def sums_of(flags, own, first, second, near_a, near_b, far4, far8, pairs, grad_query, weights, before, start, patches,
            head_size):
    _, width, rows = own.shape
    tile = 2 * LANES if rows % (2 * LANES) == 0 and start % (2 * LANES) == 0 else LANES
    chunk, whole = columns(width, tile), columns(width, tile, start // tile)
    pair = pl.BlockSpec((2 * HEADS, tile), lambda i: (0, i))
    anywhere = pl.BlockSpec(memory_space=pl.ANY)
    specs = [SMEM, chunk, whole, chunk, whole, chunk, chunk, chunk] + [pair] * 5
    specs += [pl.BlockSpec((width, tile), lambda i: (0, i))] + [anywhere] * 3
    operands = [flags, own, first, second, near_a, near_b, far4, far8, *pairs, grad_query, *weights]
    aliases = {}
    if before is not None:
        aliases = {len(operands): 0}
        specs.append(anywhere)
        operands.append(before)
    return pl.pallas_call(
        functools.partial(sum_kernel, head_size),
        grid=(rows // tile,),
        in_specs=specs,
        out_specs=pl.BlockSpec((tile, width), lambda i: (i + start // tile, 0)),
        out_shape=jax.ShapeDtypeStruct((patches, width), jnp.bfloat16),
        scratch_shapes=[pltpu.VMEM((width, tile), jnp.bfloat16)] * 2 + [pltpu.VMEM(w.shape, w.dtype) for w in weights]
        + [pltpu.SemaphoreType.DMA((3,))],
        input_output_aliases=aliases,
        compiler_params=params(),
        cost_estimate=pl.CostEstimate(flops=rows * width * 8000, bytes_accessed=rows * width * 36, transcendentals=0),
        name="sums",
    )(*operands)


def per_device(queries, keys, values, grad_out, links, w_query, w_key, w_value):
    _, patches, width = queries.shape
    head_size = width // HEADS
    me = lax.axis_index("frame")
    bit0 = lax.rem(me, 2)
    bit1 = lax.rem(me // 2, 2)
    flags = jnp.concatenate([links[0].astype(jnp.int32), jnp.stack([bit1, bit0]).astype(jnp.int32)])

    unit = patches // sum(CHUNKS)
    bounds = [0]
    for c in CHUNKS:
        bounds.append(bounds[-1] + c * unit)
    n_chunks = len(CHUNKS)

    key_value, query_grad, y_out, c_out = pack(flags, queries, keys, values, grad_out, bounds)
    up4 = [shift(kv, 4) for kv in key_value]
    down4 = [shift(qg, -4) for qg in query_grad]
    y_own = swap(y_out, 2)
    c_own = swap(c_out, 1)
    up8 = [shift(a, 4) for a in up4]
    down8 = [shift(a, -4) for a in down4]
    y_far = [swap(jnp.where(bit1 == 0, d, u), 2) for d, u in zip(down4, up4)]
    c_far = [swap(jnp.where(bit0 == bit1, y_own[:, :, bounds[i]:bounds[i + 1]], y_far[i]), 1) for i in range(n_chunks)]
    out = None
    for i in range(n_chunks):
        middle = (y_own, y_far[i], c_own, c_far[i])
        self_pair, pair1, pair2, pair4, pair8, grad_query = scores_of(
            flags, query_grad[i], key_value[i], *middle, up4[i], up8[i], bounds[i], head_size)
        came = [shift(p, -d) for p, d in ((pair1, 1), (pair2, 2), (pair4, 4), (pair8, 8))]
        out = sums_of(flags, query_grad[i], *middle, down4[i], down8[i], [self_pair, *came], grad_query,
                      (w_query, w_key, w_value), out, bounds[i], patches, head_size)
    return out[None]


def solution(mesh):
    by_frame = P(("dom", "frame"), None, None)
    return jax.shard_map(
        per_device,
        mesh=mesh,
        in_specs=(by_frame,) * 4 + (P(("dom", "frame"), None), P(), P(), P()),
        out_specs=by_frame,
        check_vma=False,
    )
```

```python
import functools

import jax
import jax.numpy as jnp
from jax import lax
from jax.experimental import pallas as pl
from jax.experimental.pallas import tpu as pltpu
from jax.sharding import PartitionSpec as P

HEADS = 16
NDIL = 4
LANES = 128
SUBLANES = 8
UNIT = 256
VMEM_BYTES = 32 * 2**20
PACK_VMEM_BYTES = 60 * 2**20


def shift(block, distance):
    n = lax.axis_size("frame")
    return lax.ppermute(block, "frame", [(i, i + distance) for i in range(n) if 0 <= i + distance < n])


def swap(block, bit):
    n = lax.axis_size("frame")
    return lax.ppermute(block, "frame", [(i, i ^ bit) for i in range(n)])


def place_bit(bit):
    return lax.rem(lax.axis_index("frame") // 2**bit, 2)


def params():
    return pltpu.CompilerParams(vmem_limit_bytes=VMEM_BYTES)


SMEM = pl.BlockSpec(memory_space=pltpu.SMEM)
VMEM = pl.BlockSpec(memory_space=pltpu.VMEM)
PIN = False


def columns(width, tile, offset=0):
    return pl.BlockSpec((2, width, tile), lambda i: (0, 0, i + offset))


def after(block, *done):
    return lax.optimization_barrier((block, *done))[0]


def pack(queries, keys, values, grad_out):
    _, patches, width = queries.shape
    tile = LANES
    steps = patches // tile
    half = steps // 2

    def kernel(q_ref, k_ref, v_ref, g_ref, kv0, kv1, qg0, qg1, y_out):
        step = pl.program_id(0)
        unit = jnp.where(lax.broadcasted_iota(jnp.int32, (UNIT, UNIT), 0) == lax.broadcasted_iota(
            jnp.int32, (UNIT, UNIT), 1), 1.0, 0.0).astype(jnp.bfloat16)

        def turned(ref):
            blocks = [lax.dot_general(unit, ref[0, :, i:i + UNIT], (((1,), (1,)), ((), ())),
                                      preferred_element_type=jnp.float32) for i in range(0, width, UNIT)]
            return jnp.concatenate([b.astype(jnp.bfloat16) for b in blocks], axis=0)

        kv = [turned(r) for r in (k_ref, v_ref)]
        qg = [turned(r) for r in (q_ref, g_ref)]
        for kv_out, qg_out, mine in ((kv0, qg0, step < half), (kv1, qg1, step >= half)):
            @pl.when(mine)
            def _(kv_out=kv_out, qg_out=qg_out):
                for part in range(2):
                    kv_out[part] = kv[part]
                    qg_out[part] = qg[part]
        for part in range(2):
            y_out[part] = jnp.where(place_bit(1) == 0, kv[part], qg[part])

    first = pl.BlockSpec((2, width, tile), lambda i: (0, 0, jnp.minimum(i, half - 1)))
    second = pl.BlockSpec((2, width, tile), lambda i: (0, 0, jnp.maximum(i - half, 0)))
    half_shape = jax.ShapeDtypeStruct((2, width, patches // 2), jnp.bfloat16)
    whole_shape = jax.ShapeDtypeStruct((2, width, patches), jnp.bfloat16)
    return pl.pallas_call(
        kernel,
        grid=(steps,),
        in_specs=[pl.BlockSpec((1, tile, width), lambda i: (0, i, 0))] * 4,
        out_specs=[first, second] * 2 + [columns(width, tile)],
        out_shape=[half_shape] * 4 + [whole_shape],
        compiler_params=pltpu.CompilerParams(vmem_limit_bytes=PACK_VMEM_BYTES),
        name="pack",
    )(queries, keys, values, grad_out)


def in_vmem(arrays):
    return [pltpu.with_memory_space_constraint(a, pltpu.VMEM) for a in arrays] if PIN else list(arrays)


def source_getters(own, y_own, y_far, c_own, c_far, far4, far8, wanted, here, there):
    def pick(first, second, bit, place):
        use_first = place_bit(bit) == wanted
        return lambda i, rows: jnp.where(use_first, first[i, rows, place], second[i, rows, here])

    return (
        lambda i, rows: own[i, rows, here],
        pick(c_own, c_far, 0, here),
        pick(y_own, y_far, 1, there),
        lambda i, rows: far4[i, rows, here],
        lambda i, rows: far8[i, rows, here],
    )


def head_slices(width):
    size = width // HEADS
    return [slice(h * size, (h + 1) * size) for h in range(HEADS)]


def lanes(step, start):
    here = pl.ds(pl.multiple_of(step * LANES, LANES), LANES)
    return here, pl.ds(pl.multiple_of(step * LANES + start, LANES), LANES)


def score_kernel(start, links, qg, own, y_own, y_far, c_own, c_far, far4, far8, self_pair, pair1, pair2, pair4, pair8,
                 grad_query, score_ref, prob_ref):
    _, width, patches = own.shape
    scale = (width // HEADS) ** (-0.5)
    pairs = (self_pair, pair1, pair2, pair4, pair8)

    @pl.loop(0, patches // LANES)
    def _(step):
        here, there = lanes(step, start)
        getters = source_getters(own, y_own, y_far, c_own, c_far, far4, far8, 1, here, there)
        for h, rows in enumerate(head_slices(width)):
            for part, into in ((0, score_ref), (1, prob_ref)):
                mine = qg[part, rows, here].astype(jnp.float32)
                for slot, get in enumerate(getters):
                    product = mine * get(part, rows).astype(jnp.float32)
                    into[slot, h * SUBLANES:(h + 1) * SUBLANES, :] = jnp.sum(
                        product.reshape(-1, SUBLANES, LANES), axis=0)

        def total_of(ref, slot):
            parts = [ref[slot, pl.ds(i, HEADS, stride=SUBLANES), :] for i in range(SUBLANES)]
            while len(parts) > 1:
                parts = [a + b for a, b in zip(parts[::2], parts[1::2])]
            return parts[0]

        scores = [total_of(score_ref, slot) * scale for slot in range(NDIL + 1)]
        scores = scores[:1] + [jnp.where(links[0, j] > 0, s, -1e30) for j, s in enumerate(scores[1:])]
        highest = functools.reduce(jnp.maximum, scores)
        raw = [jnp.exp(s - highest) for s in scores]
        raw = raw[:1] + [jnp.where(links[0, j] > 0, r, 0.0) for j, r in enumerate(raw[1:])]
        total = functools.reduce(jnp.add, raw)
        probability = [r / total for r in raw]
        grad_probs = [total_of(prob_ref, slot) for slot in range(NDIL + 1)]
        inner = functools.reduce(jnp.add, [p * g for p, g in zip(probability, grad_probs)])
        for slot, (p, g) in enumerate(zip(probability, grad_probs)):
            pairs[slot][:HEADS, here] = p * (g - inner) * scale
            pairs[slot][HEADS:, here] = p
        for h, rows in enumerate(head_slices(width)):
            terms = [pairs[s][h:h + 1, here] * get(0, rows).astype(jnp.float32) for s, get in enumerate(getters)]
            grad_query[rows, here] = functools.reduce(jnp.add, terms).astype(jnp.bfloat16)


def scores_of(links, qg, own, two, one, far4, far8, start):
    _, width, rows = own.shape
    pair_shape = jax.ShapeDtypeStruct((2 * HEADS, rows), jnp.float32)
    return pl.pallas_call(
        functools.partial(score_kernel, start),
        in_specs=[SMEM] + [VMEM] * 8,
        out_specs=[VMEM] * 6,
        out_shape=[pair_shape] * 5 + [jax.ShapeDtypeStruct((width, rows), jnp.bfloat16)],
        scratch_shapes=[pltpu.VMEM((NDIL + 1, HEADS * SUBLANES, LANES), jnp.float32)] * 2,
        compiler_params=params(),
        cost_estimate=pl.CostEstimate(flops=rows * width * 100, bytes_accessed=rows * width * 36, transcendentals=0),
        name="scores",
    )(links, *in_vmem([qg, own, *two, *one, far4, far8]))


def project_kernel(grad_query, w_query, out):
    out[...] = jnp.dot(w_query[...], grad_query[...], preferred_element_type=jnp.float32)


def project(grad_query, w_query):
    width, rows = grad_query.shape
    return pl.pallas_call(
        project_kernel,
        in_specs=[VMEM] * 2,
        out_specs=VMEM,
        out_shape=jax.ShapeDtypeStruct((w_query.shape[0], rows), jnp.float32),
        compiler_params=params(),
        cost_estimate=pl.CostEstimate(flops=2 * rows * w_query.size, bytes_accessed=2 * w_query.size, transcendentals=0),
        name="project",
    )(*in_vmem([grad_query, w_query]))


def sum_kernel(start, own, y_own, y_far, c_own, c_far, far4, far8, self_pair, pair1, pair2, pair4, pair8,
               query_part, w_key, w_value, *rest):
    out, key_ref, value_ref, result, sem = rest[-5:]
    _, width, patches = own.shape
    pairs = (self_pair, pair1, pair2, pair4, pair8)

    @pl.loop(0, patches // LANES)
    def _(step):
        here, there = lanes(step, start)
        getters = source_getters(own, y_own, y_far, c_own, c_far, far4, far8, 0, here, there)
        for h, rows in enumerate(head_slices(width)):
            for part, into in ((0, key_ref), (1, value_ref)):
                row = part * HEADS + h
                terms = [pairs[s][row:row + 1, here] * get(part, rows).astype(jnp.float32) for s, get in enumerate(getters)]
                into[rows, here] = functools.reduce(jnp.add, terms).astype(jnp.bfloat16)

    total = query_part[...] + jnp.dot(w_key[...], key_ref[...], preferred_element_type=jnp.float32)
    total = total + jnp.dot(w_value[...], value_ref[...], preferred_element_type=jnp.float32)
    result[...] = total.astype(jnp.bfloat16).T
    copy = pltpu.make_async_copy(result, out.at[pl.ds(start, patches), :], sem)
    copy.start()
    copy.wait()


def sums_of(own, two, one, far4, far8, pairs, query_part, weights, before, start, patches):
    _, width, rows = own.shape
    anywhere = pl.BlockSpec(memory_space=pl.ANY)
    operands = [*in_vmem([own, *two, *one, far4, far8, *pairs, query_part, *weights])]
    specs = [VMEM] * len(operands)
    aliases = {}
    if before is not None:
        aliases = {len(operands): 0}
        specs.append(anywhere)
        operands.append(before)
    return pl.pallas_call(
        functools.partial(sum_kernel, start),
        in_specs=specs,
        out_specs=anywhere,
        out_shape=jax.ShapeDtypeStruct((patches, width), jnp.bfloat16),
        scratch_shapes=[pltpu.VMEM((width, rows), jnp.bfloat16)] * 2
        + [pltpu.VMEM((rows, width), jnp.bfloat16), pltpu.SemaphoreType.DMA],
        input_output_aliases=aliases,
        compiler_params=params(),
        cost_estimate=pl.CostEstimate(flops=rows * width * 8000, bytes_accessed=rows * width * 36, transcendentals=0),
        name="sums",
    )(*operands)


def per_device(queries, keys, values, grad_out, links, w_query, w_key, w_value):
    patches = queries.shape[1]
    bit0, bit1 = place_bit(0), place_bit(1)
    half = patches // 2

    def choose(bit, if_set, if_clear):
        return jnp.where(bit == 1, if_set, if_clear)

    kv0, kv1, qg0, qg1, y_own = pack(queries, keys, values, grad_out)
    y_own = swap(y_own, 2)
    up4_0, down4_0 = shift(kv0, 4), shift(qg0, -4)
    up4_1, down4_1 = shift(kv1, 4), shift(qg1, -4)
    up8_0, down8_0 = shift(after(up4_0, down4_0), 4), shift(after(down4_0, up4_0), -4)
    y_far0 = swap(after(choose(bit1, up4_0, down4_0), up4_1, down4_1), 2)
    up8_1, down8_1 = shift(after(up4_1, y_own), 4), shift(after(down4_1, y_own), -4)
    y_far1 = swap(after(choose(bit1, up4_1, down4_1), y_far0, up8_0, down8_0), 2)
    c_own0 = swap(after(choose(bit0, qg0, kv0), up8_0, down8_0), 1)
    c_own1 = swap(after(choose(bit0, qg1, kv1), up8_1, down8_1), 1)

    def near(y_own, y_far):
        return choose(bit0, choose(bit1, y_own, y_far), choose(bit1, y_far, y_own))

    def pairs_back(pair8, pair4, pair2, pair1):
        return [shift(p, -d) for p, d in ((pair8, 8), (pair4, 4), (pair2, 2), (pair1, 1))]

    c_far0 = swap(near(y_own[:, :, :half], after(y_far0, c_own0)), 1)
    two, one = (y_own, y_far0), (c_own0, c_far0)
    self0, pair1, pair2, pair4, pair8, grad_query0 = scores_of(links, qg0, kv0, two, one, up4_0, up8_0, 0)
    came0 = pairs_back(pair8, pair4, pair2, pair1)
    query_part0 = project(grad_query0, w_query)
    c_far1 = swap(near(y_own[:, :, half:], after(y_far1, c_own1, pair8)), 1)
    near0 = two, one
    two, one = (y_own, y_far1), (c_own1, c_far1)
    self1, pair1, pair2, pair4, pair8, grad_query1 = scores_of(links, qg1, kv1, two, one, up4_1, up8_1, half)
    came1 = pairs_back(pair8, pair4, pair2, pair1)
    out = sums_of(after(qg0, pair8), *near0, down4_0, down8_0, [self0, *came0[::-1]], query_part0, (w_key, w_value), None, 0,
                  patches)
    query_part1 = project(grad_query1, w_query)
    out = sums_of(qg1, two, one, down4_1, down8_1, [self1, *came1[::-1]], query_part1, (w_key, w_value), out, half,
                  patches)
    return out[None]


def solution(mesh):
    by_frame = P(("dom", "frame"), None, None)
    return jax.shard_map(
        per_device,
        mesh=mesh,
        in_specs=(by_frame,) * 4 + (P(("dom", "frame"), None), P(), P(), P()),
        out_specs=by_frame,
        check_vma=False,
    )
```

```python
import functools

import jax
import jax.numpy as jnp
from jax import lax
from jax.experimental import pallas as pl
from jax.experimental.pallas import tpu as pltpu
from jax.sharding import PartitionSpec as P

HEADS = 16
NDIL = 4
LANES = 128
SUBLANES = 8
HEAVY = 48
VMEM_BYTES = 32 * 2**20


def shift(block, distance):
    n = lax.axis_size("frame")
    return lax.ppermute(block, "frame", [(i, i + distance) for i in range(n) if 0 <= i + distance < n])


def swap(block, bit):
    n = lax.axis_size("frame")
    return lax.ppermute(block, "frame", [(i, i ^ bit) for i in range(n)])


def place_bit(bit):
    return lax.rem(lax.axis_index("frame") // 2**bit, 2)


def params():
    return pltpu.CompilerParams(vmem_limit_bytes=VMEM_BYTES)


SMEM = pl.BlockSpec(memory_space=pltpu.SMEM)
VMEM = pl.BlockSpec(memory_space=pltpu.VMEM)
PIN = False


def after(block, *done):
    return lax.optimization_barrier((block, *done))[0]


def pack(queries, keys, values, grad_out):
    _, patches, width = queries.shape
    half = patches // 2

    def kernel(q_hbm, k_hbm, v_hbm, g_hbm, kv0, kv1, qg0, qg1, y_out, q_ref, k_ref, v_ref, g_ref, sems):
        pieces = []
        for i in range(2):
            rows = pl.ds(i * half, half)
            for part, up, down in ((0, (k_hbm, k_ref), (q_hbm, q_ref)), (1, (v_hbm, v_ref), (g_hbm, g_ref))):
                for (hbm, ref), out, bit in ((up, (kv0, kv1)[i], 0), (down, (qg0, qg1)[i], 1)):
                    copy = pltpu.make_async_copy(hbm.at[0, rows, :], ref.at[rows, :], sems.at[len(pieces)])
                    pieces.append((copy, ref, i * half, out, part, bit))
        for piece in pieces:
            piece[0].start()
        for copy, ref, start, out, part, bit in pieces:
            copy.wait()
            for p in range(0, half, LANES):
                turned = ref[start + p:start + p + LANES, :].T
                out[part, :, p:p + LANES] = turned

                @pl.when(place_bit(1) == bit)
                def _():
                    y_out[part, :, start + p:start + p + LANES] = turned

    half_shape = jax.ShapeDtypeStruct((2, width, half), jnp.bfloat16)
    whole_shape = jax.ShapeDtypeStruct((2, width, patches), jnp.bfloat16)
    return pl.pallas_call(
        kernel,
        in_specs=[pl.BlockSpec(memory_space=pl.ANY)] * 4,
        out_specs=[VMEM] * 5,
        out_shape=[half_shape] * 4 + [whole_shape],
        scratch_shapes=[pltpu.VMEM((patches, width), jnp.bfloat16)] * 4 + [pltpu.SemaphoreType.DMA((8,))],
        compiler_params=params(),
        name="pack",
    )(*(pltpu.with_memory_space_constraint(a, pltpu.HBM) for a in (queries, keys, values, grad_out)))


def pick(test, if_true, if_false, start=0, weight=1):
    def kernel(a_ref, b_ref, out):
        chosen = test()

        @pl.when(chosen)
        def _():
            out[...] = a_ref[:, :, start:start + out.shape[2]]

        @pl.when(jnp.logical_not(chosen))
        def _():
            out[...] = b_ref[...]

    return pl.pallas_call(
        kernel,
        in_specs=[VMEM] * 2,
        out_specs=VMEM,
        out_shape=jax.ShapeDtypeStruct(if_false.shape, if_false.dtype),
        compiler_params=params(),
        cost_estimate=pl.CostEstimate(flops=0, bytes_accessed=weight * if_false.size, transcendentals=0),
        name="pick",
    )(if_true, if_false)


def in_vmem(arrays):
    return [pltpu.with_memory_space_constraint(a, pltpu.VMEM) for a in arrays] if PIN else list(arrays)


def source_getters(own, y_own, y_far, c_own, c_far, far4, far8, wanted, here, there):
    def pick(first, second, bit, place):
        use_first = place_bit(bit) == wanted
        return lambda i, rows: jnp.where(use_first, first[i, rows, place], second[i, rows, here])

    return (
        lambda i, rows: own[i, rows, here],
        pick(c_own, c_far, 0, here),
        pick(y_own, y_far, 1, there),
        lambda i, rows: far4[i, rows, here],
        lambda i, rows: far8[i, rows, here],
    )


def head_slices(width):
    size = width // HEADS
    return [slice(h * size, (h + 1) * size) for h in range(HEADS)]


def lanes(step, start):
    here = pl.ds(pl.multiple_of(step * LANES, LANES), LANES)
    return here, pl.ds(pl.multiple_of(step * LANES + start, LANES), LANES)


def score_kernel(start, links, qg, own, y_own, y_far, c_own, c_far, far4, far8, self_pair, pair1, pair2, pair4, pair8,
                 grad_query, score_ref, prob_ref):
    _, width, patches = own.shape
    scale = (width // HEADS) ** (-0.5)
    pairs = (self_pair, pair1, pair2, pair4, pair8)

    @pl.loop(0, patches // LANES)
    def _(step):
        here, there = lanes(step, start)
        getters = source_getters(own, y_own, y_far, c_own, c_far, far4, far8, 1, here, there)
        for h, rows in enumerate(head_slices(width)):
            for part, into in ((0, score_ref), (1, prob_ref)):
                mine = qg[part, rows, here].astype(jnp.float32)
                for slot, get in enumerate(getters):
                    product = mine * get(part, rows).astype(jnp.float32)
                    into[slot, h * SUBLANES:(h + 1) * SUBLANES, :] = jnp.sum(
                        product.reshape(-1, SUBLANES, LANES), axis=0)

        def total_of(ref, slot):
            parts = [ref[slot, pl.ds(i, HEADS, stride=SUBLANES), :] for i in range(SUBLANES)]
            while len(parts) > 1:
                parts = [a + b for a, b in zip(parts[::2], parts[1::2])]
            return parts[0]

        scores = [total_of(score_ref, slot) * scale for slot in range(NDIL + 1)]
        scores = scores[:1] + [jnp.where(links[0, j] > 0, s, -1e30) for j, s in enumerate(scores[1:])]
        highest = functools.reduce(jnp.maximum, scores)
        raw = [jnp.exp(s - highest) for s in scores]
        raw = raw[:1] + [jnp.where(links[0, j] > 0, r, 0.0) for j, r in enumerate(raw[1:])]
        total = functools.reduce(jnp.add, raw)
        probability = [r / total for r in raw]
        grad_probs = [total_of(prob_ref, slot) for slot in range(NDIL + 1)]
        inner = functools.reduce(jnp.add, [p * g for p, g in zip(probability, grad_probs)])
        for slot, (p, g) in enumerate(zip(probability, grad_probs)):
            pairs[slot][:HEADS, here] = p * (g - inner) * scale
            pairs[slot][HEADS:, here] = p
        for h, rows in enumerate(head_slices(width)):
            terms = [pairs[s][h:h + 1, here] * get(0, rows).astype(jnp.float32) for s, get in enumerate(getters)]
            grad_query[rows, here] = functools.reduce(jnp.add, terms).astype(jnp.bfloat16)


def scores_of(links, qg, own, two, one, far4, far8, start, weight):
    _, width, rows = own.shape
    pair_shape = jax.ShapeDtypeStruct((2 * HEADS, rows), jnp.float32)
    return pl.pallas_call(
        functools.partial(score_kernel, start),
        in_specs=[SMEM] + [VMEM] * 8,
        out_specs=[VMEM] * 6,
        out_shape=[pair_shape] * 5 + [jax.ShapeDtypeStruct((width, rows), jnp.bfloat16)],
        scratch_shapes=[pltpu.VMEM((NDIL + 1, HEADS * SUBLANES, LANES), jnp.float32)] * 2,
        compiler_params=params(),
        cost_estimate=pl.CostEstimate(flops=0, bytes_accessed=weight * rows * width, transcendentals=0),
        name="scores",
    )(links, *in_vmem([qg, own, *two, *one, far4, far8]))


def project_kernel(grad_query, w_query, out):
    out[...] = jnp.dot(w_query[...], grad_query[...], preferred_element_type=jnp.float32)


def project(grad_query, w_query):
    width, rows = grad_query.shape
    return pl.pallas_call(
        project_kernel,
        in_specs=[VMEM] * 2,
        out_specs=VMEM,
        out_shape=jax.ShapeDtypeStruct((w_query.shape[0], rows), jnp.float32),
        compiler_params=params(),
        cost_estimate=pl.CostEstimate(flops=2 * rows * w_query.size, bytes_accessed=2 * w_query.size, transcendentals=0),
        name="project",
    )(*in_vmem([grad_query, w_query]))


def sum_kernel(start, own, y_own, y_far, c_own, c_far, far4, far8, self_pair, pair1, pair2, pair4, pair8,
               query_part, w_key, w_value, *rest):
    out, key_ref, value_ref, result, sem = rest[-5:]
    _, width, patches = own.shape
    pairs = (self_pair, pair1, pair2, pair4, pair8)

    @pl.loop(0, patches // LANES)
    def _(step):
        here, there = lanes(step, start)
        getters = source_getters(own, y_own, y_far, c_own, c_far, far4, far8, 0, here, there)
        for h, rows in enumerate(head_slices(width)):
            for part, into in ((0, key_ref), (1, value_ref)):
                row = part * HEADS + h
                terms = [pairs[s][row:row + 1, here] * get(part, rows).astype(jnp.float32) for s, get in enumerate(getters)]
                into[rows, here] = functools.reduce(jnp.add, terms).astype(jnp.bfloat16)

    total = query_part[...] + jnp.dot(w_key[...], key_ref[...], preferred_element_type=jnp.float32)
    total = total + jnp.dot(w_value[...], value_ref[...], preferred_element_type=jnp.float32)
    result[...] = total.astype(jnp.bfloat16).T
    copy = pltpu.make_async_copy(result, out.at[pl.ds(start, patches), :], sem)
    copy.start()
    copy.wait()


def sums_of(own, two, one, far4, far8, pairs, query_part, weights, before, start, patches):
    _, width, rows = own.shape
    anywhere = pl.BlockSpec(memory_space=pl.ANY)
    operands = [*in_vmem([own, *two, *one, far4, far8, *pairs, query_part, *weights])]
    specs = [VMEM] * len(operands)
    aliases = {}
    if before is not None:
        aliases = {len(operands): 0}
        specs.append(anywhere)
        operands.append(before)
    return pl.pallas_call(
        functools.partial(sum_kernel, start),
        in_specs=specs,
        out_specs=anywhere,
        out_shape=jax.ShapeDtypeStruct((patches, width), jnp.bfloat16),
        scratch_shapes=[pltpu.VMEM((width, rows), jnp.bfloat16)] * 2
        + [pltpu.VMEM((rows, width), jnp.bfloat16), pltpu.SemaphoreType.DMA],
        input_output_aliases=aliases,
        compiler_params=params(),
        cost_estimate=pl.CostEstimate(flops=rows * width * 8000, bytes_accessed=rows * width * 36, transcendentals=0),
        name="sums",
    )(*operands)


def per_device(queries, keys, values, grad_out, links, w_query, w_key, w_value):
    patches = queries.shape[1]
    half = patches // 2

    def upper(bit):
        return lambda: place_bit(bit) == 1

    def same_bits():
        return place_bit(0) == place_bit(1)

    kv0, kv1, qg0, qg1, y_own = pack(queries, keys, values, grad_out)
    y_own = swap(y_own, 2)
    up4_0, down4_0 = shift(kv0, 4), shift(qg0, -4)
    up4_1, down4_1 = shift(kv1, 4), shift(qg1, -4)
    up8_0, down8_0 = shift(after(up4_0, down4_0), 4), shift(after(down4_0, up4_0), -4)
    y_far0 = swap(pick(upper(1), up4_0, down4_0), 2)
    up8_1, down8_1 = shift(after(up4_1, y_own), 4), shift(after(down4_1, y_own), -4)
    y_far1 = swap(after(pick(upper(1), up4_1, down4_1), up8_0, down8_0), 2)
    c_own0 = swap(after(pick(upper(0), qg0, kv0), up8_0, down8_0), 1)
    c_own1 = swap(after(pick(upper(0), qg1, kv1), up8_1, down8_1), 1)

    def pairs_back(pair8, pair4, pair2, pair1):
        return [shift(p, -d) for p, d in ((pair8, 8), (pair4, 4), (pair2, 2), (pair1, 1))]

    c_far0 = swap(pick(same_bits, y_own, y_far0), 1)
    two, one = (y_own, y_far0), (c_own0, c_far0)
    self0, pair1, pair2, pair4, pair8, grad_query0 = scores_of(links, qg0, kv0, two, one, up4_0, up8_0, 0, 140)
    came0 = pairs_back(pair8, pair4, pair2, pair1)
    query_part0 = project(grad_query0, w_query)
    c_far1 = swap(after(pick(same_bits, y_own, after(y_far1, c_own1), half, HEAVY), pair8), 1)
    near0 = two, one
    two, one = (y_own, y_far1), (c_own1, c_far1)
    self1, pair1, pair2, pair4, pair8, grad_query1 = scores_of(links, qg1, kv1, two, one, up4_1, up8_1, half, 1)
    came1 = pairs_back(pair8, pair4, pair2, pair1)
    out = sums_of(after(qg0, pair8), *near0, down4_0, down8_0, [self0, *came0[::-1]], query_part0, (w_key, w_value), None, 0,
                  patches)
    query_part1 = project(grad_query1, w_query)
    out = sums_of(qg1, two, one, down4_1, down8_1, [self1, *came1[::-1]], query_part1, (w_key, w_value), out, half,
                  patches)
    return out[None]


def solution(mesh):
    by_frame = P(("dom", "frame"), None, None)
    return jax.shard_map(
        per_device,
        mesh=mesh,
        in_specs=(by_frame,) * 4 + (P(("dom", "frame"), None), P(), P(), P()),
        out_specs=by_frame,
        check_vma=False,
    )
```

```python
import functools

import jax
import jax.numpy as jnp
from jax import lax
from jax.experimental import pallas as pl
from jax.experimental.pallas import tpu as pltpu
from jax.sharding import PartitionSpec as P

HEADS = 16
NDIL = 4
LANES = 128
SUBLANES = 8
PIECE = 256
US = 3.69e6
BY_BIT0, BY_BIT1 = (0, 1, 0, 1), (0, 0, 1, 1)
VMEM_BYTES = 32 * 2**20


def shift(block, distance):
    n = lax.axis_size("frame")
    return lax.ppermute(block, "frame", [(i, i + distance) for i in range(n) if 0 <= i + distance < n])


def swap(block, bit):
    n = lax.axis_size("frame")
    return lax.ppermute(block, "frame", [(i, i ^ bit) for i in range(n)])


def place_bit(bit):
    return lax.rem(lax.axis_index("frame") // 2**bit, 2)


def params():
    return pltpu.CompilerParams(vmem_limit_bytes=VMEM_BYTES)


SMEM = pl.BlockSpec(memory_space=pltpu.SMEM)
VMEM = pl.BlockSpec(memory_space=pltpu.VMEM)


def after(block, *done):
    return lax.optimization_barrier((block, *done))[0] if done else block


def pack(queries, keys, values, grad_out):
    _, patches, width = queries.shape
    half = patches // 2

    def kernel(q_hbm, k_hbm, v_hbm, g_hbm, kv0, kv1, qg0, qg1, y_out, q_ref, k_ref, v_ref, g_ref, sems):
        pieces = []
        for i in range(2):
            rows = pl.ds(i * half, half)
            for part, up, down in ((0, (k_hbm, k_ref), (q_hbm, q_ref)), (1, (v_hbm, v_ref), (g_hbm, g_ref))):
                for (hbm, ref), out, bit in ((up, (kv0, kv1)[i], 0), (down, (qg0, qg1)[i], 1)):
                    copy = pltpu.make_async_copy(hbm.at[0, rows, :], ref.at[rows, :], sems.at[len(pieces)])
                    pieces.append((copy, ref, i * half, out, part, bit))
        for piece in pieces:
            piece[0].start()
        for copy, ref, start, out, part, bit in pieces:
            copy.wait()
            for p in range(0, half, LANES):
                turned = ref[start + p:start + p + LANES, :].T
                out[part, :, p:p + LANES] = turned

                if start == 0:
                    @pl.when(place_bit(1) == bit)
                    def _():
                        y_out[part, :, p:p + LANES] = turned

    half_shape = jax.ShapeDtypeStruct((2, width, half), jnp.bfloat16)
    return pl.pallas_call(
        kernel,
        in_specs=[pl.BlockSpec(memory_space=pl.ANY)] * 4,
        out_specs=[VMEM] * 5,
        out_shape=[half_shape] * 5,
        scratch_shapes=[pltpu.VMEM((patches, width), jnp.bfloat16)] * 4 + [pltpu.SemaphoreType.DMA((8,))],
        compiler_params=params(),
        name="pack",
    )(*(pltpu.with_memory_space_constraint(a, pltpu.HBM) for a in (queries, keys, values, grad_out)))


def pick(blocks, which, weight=1):
    def kernel(*refs):
        place = 2 * place_bit(1) + place_bit(0)
        for number, ref in enumerate(refs[:-1]):
            mine = [place == p for p in range(4) if which[p] == number]

            @pl.when(functools.reduce(jnp.logical_or, mine))
            def _(ref=ref):
                refs[-1][...] = ref[...]

    size = blocks[0].size
    return pl.pallas_call(
        kernel,
        in_specs=[VMEM] * len(blocks),
        out_specs=VMEM,
        out_shape=jax.ShapeDtypeStruct(blocks[0].shape, blocks[0].dtype),
        compiler_params=params(),
        cost_estimate=pl.CostEstimate(flops=0, bytes_accessed=int(weight * US), transcendentals=0),
        name="pick",
    )(*blocks)


def choose(blocks, bit, wanted, here):
    if len(blocks) == 1:
        return lambda i, rows: blocks[0][i, rows, here]
    use_first = place_bit(bit) == wanted
    return lambda i, rows: jnp.where(use_first, blocks[0][i, rows, here], blocks[1][i, rows, here])


def source_getters(own, two, one, far4, far8, wanted, here):
    return (
        choose([own], 0, wanted, here),
        choose(one, 0, wanted, here),
        choose(two, 1, wanted, here),
        choose([far4], 0, wanted, here),
        choose([far8], 0, wanted, here),
    )


def head_slices(width):
    size = width // HEADS
    return [slice(h * size, (h + 1) * size) for h in range(HEADS)]


def lanes(step):
    return pl.ds(pl.multiple_of(step * LANES, LANES), LANES)


def head_products(mine, other, part, here, into):
    for h, rows in enumerate(head_slices(mine.shape[1])):
        left = mine[part, rows, here].astype(jnp.float32)
        for slot, get in enumerate(other):
            product = left * get(part, rows).astype(jnp.float32)
            into[slot, h * SUBLANES:(h + 1) * SUBLANES, :] = jnp.sum(product.reshape(-1, SUBLANES, LANES), axis=0)


def sublane_total(ref, slot):
    parts = [ref[slot, pl.ds(i, HEADS, stride=SUBLANES), :] for i in range(SUBLANES)]
    while len(parts) > 1:
        parts = [a + b for a, b in zip(parts[::2], parts[1::2])]
    return parts[0]


def product_kernel(n_two, n_one, n_other, qg, *rest):
    *sources, out, work = rest
    others = sources[:n_other]
    two, one = sources[n_other:n_other + n_two], sources[n_other + n_two:]

    @pl.loop(0, qg.shape[2] // LANES)
    def _(step):
        here = lanes(step)
        getters = [choose([o], 0, 1, here) for o in others]
        getters += [choose(blocks, bit, 1, here) for blocks, bit in ((one, 0), (two, 1)) if blocks]
        for part in range(2):
            head_products(qg, getters, part, here, work)
            for slot in range(len(getters)):
                out[part, slot, :, here] = sublane_total(work, slot)


def products_of(qg, others, two, one, weight):
    rows = qg.shape[2]
    slots = len(others) + bool(two) + bool(one)
    return pl.pallas_call(
        functools.partial(product_kernel, len(two), len(one), len(others)),
        in_specs=[VMEM] * (1 + len(others) + len(two) + len(one)),
        out_specs=VMEM,
        out_shape=jax.ShapeDtypeStruct((2, slots, HEADS, rows), jnp.float32),
        scratch_shapes=[pltpu.VMEM((slots, HEADS * SUBLANES, LANES), jnp.float32)],
        compiler_params=params(),
        cost_estimate=pl.CostEstimate(flops=0, bytes_accessed=int(weight * US), transcendentals=0),
        name="products",
    )(qg, *others, *two, *one)


def score_kernel(head_size, links, near0, near1, far0, far1, self_pair, pair1, pair2, pair4, pair8):
    scale = head_size ** (-0.5)
    half = far0.shape[-1]
    for start, near, far in ((0, near0, far0), (half, near1, far1)):
        here = slice(start, start + half)
        products = [[near[part, 0], near[part, 2], near[part, 3], near[part, 1], far[part, 0]] for part in range(2)]
        scores = [p * scale for p in products[0]]
        scores = scores[:1] + [jnp.where(links[0, j] > 0, s, -1e30) for j, s in enumerate(scores[1:])]
        highest = functools.reduce(jnp.maximum, scores)
        raw = [jnp.exp(s - highest) for s in scores]
        raw = raw[:1] + [jnp.where(links[0, j] > 0, r, 0.0) for j, r in enumerate(raw[1:])]
        total = functools.reduce(jnp.add, raw)
        probability = [r / total for r in raw]
        inner = functools.reduce(jnp.add, [p * g for p, g in zip(probability, products[1])])
        for pair, p, g in zip((self_pair, pair1, pair2, pair4, pair8), probability, products[1]):
            pair[:HEADS, here] = p * (g - inner) * scale
            pair[HEADS:, here] = p


def scores_of(links, near0, near1, far0, far1, head_size, weight):
    pair = jax.ShapeDtypeStruct((2 * HEADS, 2 * far0.shape[-1]), jnp.float32)
    return pl.pallas_call(
        functools.partial(score_kernel, head_size),
        in_specs=[SMEM] + [VMEM] * 4,
        out_specs=[VMEM] * 5,
        out_shape=[pair] * 5,
        compiler_params=params(),
        cost_estimate=pl.CostEstimate(flops=0, bytes_accessed=int(weight * US), transcendentals=0),
        name="scores",
    )(links, near0, near1, far0, far1)


def query_kernel(start, own, two_a, two_b, one_a, one_b, far4, far8, self_pair, pair1, pair2, pair4, pair8, w_query, out,
                 grad_query):
    _, width, patches = own.shape
    pairs = (self_pair, pair1, pair2, pair4, pair8)

    @pl.loop(0, patches // LANES)
    def _(step):
        here = lanes(step)
        there = lanes(step + start // LANES)
        getters = source_getters(own, (two_a, two_b), (one_a, one_b), far4, far8, 1, here)
        for h, rows in enumerate(head_slices(width)):
            terms = [pairs[s][h:h + 1, there] * get(0, rows).astype(jnp.float32) for s, get in enumerate(getters)]
            grad_query[rows, here] = functools.reduce(jnp.add, terms).astype(jnp.bfloat16)

    out[...] = jnp.dot(w_query[...], grad_query[...], preferred_element_type=jnp.float32)


def query_part_of(own, two, one, far4, far8, pairs, w_query, start, weight):
    _, width, rows = own.shape
    return pl.pallas_call(
        functools.partial(query_kernel, start),
        in_specs=[VMEM] * 13,
        out_specs=VMEM,
        out_shape=jax.ShapeDtypeStruct((w_query.shape[0], rows), jnp.float32),
        scratch_shapes=[pltpu.VMEM((width, rows), jnp.bfloat16)],
        compiler_params=params(),
        cost_estimate=pl.CostEstimate(flops=0, bytes_accessed=int(weight * US), transcendentals=0),
        name="query_part",
    )(own, *two, *one, far4, far8, *pairs, w_query)


def sum_kernel(shapes, self_pair, pair8, pair4, pair2, pair1, w_key, w_value, *rest):
    out, key_ref, value_ref, result, sems = rest[-5:]
    rest = rest[:-5]
    pairs = (self_pair, pair1, pair2, pair4, pair8)
    copies = []
    for i, (n_two, n_one) in enumerate(shapes):
        own, query_part, far4, far8 = rest[:4]
        two, one, rest = rest[4:4 + n_two], rest[4 + n_two:4 + n_two + n_one], rest[4 + n_two + n_one:]
        _, width, patches = own.shape

        @pl.loop(0, patches // LANES)
        def _(step):
            here = lanes(step)
            there = lanes(step + i * (patches // LANES))
            getters = source_getters(own, two, one, far4, far8, 0, here)
            for h, rows in enumerate(head_slices(width)):
                for part, into in ((0, key_ref), (1, value_ref)):
                    row = part * HEADS + h
                    terms = [pairs[s][row:row + 1, there] * get(part, rows).astype(jnp.float32)
                             for s, get in enumerate(getters)]
                    into[rows, there] = functools.reduce(jnp.add, terms).astype(jnp.bfloat16)

        columns = pl.ds(i * patches, patches)
        for o in range(0, width, PIECE):
            piece = slice(o, o + PIECE)
            total = query_part[piece, :] + jnp.dot(
                w_key[piece, :], key_ref[:, columns], preferred_element_type=jnp.float32)
            total = total + jnp.dot(w_value[piece, :], value_ref[:, columns], preferred_element_type=jnp.float32)
            result[columns, piece] = total.astype(jnp.bfloat16).T
        copies.append(pltpu.make_async_copy(result.at[columns, :], out.at[columns, :], sems.at[i]))
        copies[-1].start()
    for copy in copies:
        copy.wait()


def sums_of(halves, pairs, weights, weight):
    _, width, rows = halves[0][0].shape
    operands = [*pairs, *weights]
    for own, query_part, two, one, far4, far8 in halves:
        operands += [own, query_part, far4, far8, *two, *one]
    return pl.pallas_call(
        functools.partial(sum_kernel, [(len(h[2]), len(h[3])) for h in halves]),
        in_specs=[VMEM] * len(operands),
        out_specs=pl.BlockSpec(memory_space=pl.ANY),
        out_shape=jax.ShapeDtypeStruct((2 * rows, width), jnp.bfloat16),
        scratch_shapes=[pltpu.VMEM((width, 2 * rows), jnp.bfloat16)] * 2
        + [pltpu.VMEM((2 * rows, width), jnp.bfloat16), pltpu.SemaphoreType.DMA((2,))],
        compiler_params=params(),
        cost_estimate=pl.CostEstimate(flops=0, bytes_accessed=int(weight * US), transcendentals=0),
        name="sums",
    )(*operands)


def per_device(queries, keys, values, grad_out, links, w_query, w_key, w_value):
    patches = queries.shape[1]
    half = patches // 2
    head_size = keys.shape[2] // HEADS
    kv0, kv1, qg0, qg1, owed = pack(queries, keys, values, grad_out)
    up4_0 = shift(kv0, 4)
    down4_0 = shift(qg0, -4)
    y_a = swap(owed, 2)
    up4_1 = shift(kv1, 4)
    down4_1 = shift(qg1, -4)
    y_b = swap(after(pick((kv1, up4_0), BY_BIT1, 0), y_a, down4_0), 2)
    up8_0 = shift(after(up4_0, down4_0), 4)
    down8_0 = shift(after(down4_0, up4_0), -4)
    c_a = swap(pick((after(kv0, up4_1, down4_1), qg0), BY_BIT0, 2.8), 1)
    y_c = swap(pick((down4_0, up4_1), BY_BIT1, 0), 2)
    up8_1 = shift(after(up4_1, y_b), 4)
    down8_1 = shift(after(down4_1, up8_0, down8_0), -4)
    c_b = swap(pick((kv1, y_b, y_a), (0, 1, 0, 2), 0), 1)
    far0 = products_of(after(qg0, down8_0), [up8_0], (), (), 5.7)
    near0 = products_of(qg0, [kv0, up4_0], (y_a, y_b), (c_a, c_b), 0)
    y_d = swap(after(pick((down4_1, qg1), BY_BIT1, 0), up8_0, down8_0), 2)
    c_c = swap(after(pick((y_a, y_c, y_b), (0, 1, 1, 2), 0), near0, far0), 1)
    near1 = products_of(qg1, [kv1, up4_1], (y_b, y_c), (c_b, c_c), 0)
    far1 = products_of(qg1, [up8_1], (), (), 10)
    pairs = scores_of(links, near0, near1, far0, far1, head_size, 0)
    self_pair, pair1, pair2, pair4, pair8 = pairs
    came8 = shift(pair8, -8)
    came4 = shift(pair4, -4)
    came2 = shift(pair2, -2)
    came1 = shift(pair1, -1)
    query_part0 = query_part_of(kv0, (y_a, y_b), (c_a, c_b), up4_0, up8_0, pairs, w_query, 0, 0)
    query_part1 = query_part_of(kv1, (y_b, y_c), (c_b, c_c), up4_1, up8_1, pairs, w_query, half, 0)
    c_d = swap(pick((y_d, qg1), BY_BIT0, 0), 1)
    halves = (
        (qg0, query_part0, (y_a, y_c), (c_a, c_c), down4_0, down8_0),
        (qg1, query_part1, (y_d,), (c_d,), down4_1, down8_1),
    )
    out = sums_of(halves, (self_pair, came8, came4, came2, came1), (w_key, w_value), 3)
    return out[None]


def solution(mesh):
    by_frame = P(("dom", "frame"), None, None)
    return jax.shard_map(
        per_device,
        mesh=mesh,
        in_specs=(by_frame,) * 4 + (P(("dom", "frame"), None), P(), P(), P()),
        out_specs=by_frame,
        check_vma=False,
    )
```

```python
import functools

import jax
import jax.numpy as jnp
from jax import lax
from jax.experimental import pallas as pl
from jax.experimental.pallas import tpu as pltpu
from jax.sharding import PartitionSpec as P

HEADS = 16
NDIL = 4
LANES = 128
SUBLANES = 8
PIECE = 256
US = 3.69e6
US_FLOPS = 1.15e9
BY_BIT0, BY_BIT1 = (0, 1, 0, 1), (0, 0, 1, 1)
VMEM_BYTES = 32 * 2**20


def shift(block, distance):
    n = lax.axis_size("frame")
    return lax.ppermute(block, "frame", [(i, i + distance) for i in range(n) if 0 <= i + distance < n])


def swap(block, bit):
    n = lax.axis_size("frame")
    return lax.ppermute(block, "frame", [(i, i ^ bit) for i in range(n)])


def place_bit(bit):
    return lax.rem(lax.axis_index("frame") // 2**bit, 2)


def params():
    return pltpu.CompilerParams(vmem_limit_bytes=VMEM_BYTES)


SMEM = pl.BlockSpec(memory_space=pltpu.SMEM)
VMEM = pl.BlockSpec(memory_space=pltpu.VMEM)


def after(block, *done):
    return lax.optimization_barrier((block, *done))[0] if done else block


def pack(queries, keys, values, grad_out, start, rows, with_owed):
    width = queries.shape[2]

    def kernel(q_hbm, k_hbm, v_hbm, g_hbm, kv_out, qg_out, *rest):
        owed, (q_ref, k_ref, v_ref, g_ref, sems) = rest[:-5], rest[-5:]
        pieces = []
        for part, up, down in ((0, (k_hbm, k_ref), (q_hbm, q_ref)), (1, (v_hbm, v_ref), (g_hbm, g_ref))):
            for (hbm, ref), out, bit in ((up, kv_out, 0), (down, qg_out, 1)):
                copy = pltpu.make_async_copy(hbm.at[0, pl.ds(start, rows), :], ref, sems.at[len(pieces)])
                pieces.append((copy, ref, out, part, bit))
        for piece in pieces:
            piece[0].start()
        for copy, ref, out, part, bit in pieces:
            copy.wait()
            for p in range(0, rows, LANES):
                turned = ref[p:p + LANES, :].T
                out[part, :, p:p + LANES] = turned
                for y_out in owed:
                    @pl.when(place_bit(1) == bit)
                    def _():
                        y_out[part, :, p:p + LANES] = turned

    shape = jax.ShapeDtypeStruct((2, width, rows), jnp.bfloat16)
    n_out = 3 if with_owed else 2
    return pl.pallas_call(
        kernel,
        in_specs=[pl.BlockSpec(memory_space=pl.ANY)] * 4,
        out_specs=[VMEM] * n_out,
        out_shape=[shape] * n_out,
        scratch_shapes=[pltpu.VMEM((rows, width), jnp.bfloat16)] * 4 + [pltpu.SemaphoreType.DMA((4,))],
        compiler_params=params(),
        name="pack",
    )(*(pltpu.with_memory_space_constraint(a, pltpu.HBM) for a in (queries, keys, values, grad_out)))


def pick(blocks, which, weight=1):
    def kernel(*refs):
        place = 2 * place_bit(1) + place_bit(0)
        for number, ref in enumerate(refs[:-1]):
            mine = [place == p for p in range(4) if which[p] == number]

            @pl.when(functools.reduce(jnp.logical_or, mine))
            def _(ref=ref):
                refs[-1][...] = ref[...]

    size = blocks[0].size
    return pl.pallas_call(
        kernel,
        in_specs=[VMEM] * len(blocks),
        out_specs=VMEM,
        out_shape=jax.ShapeDtypeStruct(blocks[0].shape, blocks[0].dtype),
        compiler_params=params(),
        cost_estimate=pl.CostEstimate(flops=int(weight * US_FLOPS), bytes_accessed=int(weight * US), transcendentals=0),
        name="pick",
    )(*blocks)


def choose(blocks, bit, wanted, here):
    if len(blocks) == 1:
        return lambda i, rows: blocks[0][i, rows, here]
    use_first = place_bit(bit) == wanted
    return lambda i, rows: jnp.where(use_first, blocks[0][i, rows, here], blocks[1][i, rows, here])


def source_getters(own, two, one, far4, far8, wanted, here):
    return (
        choose([own], 0, wanted, here),
        choose(one, 0, wanted, here),
        choose(two, 1, wanted, here),
        choose([far4], 0, wanted, here),
        choose([far8], 0, wanted, here),
    )


def head_slices(width):
    size = width // HEADS
    return [slice(h * size, (h + 1) * size) for h in range(HEADS)]


def lanes(step):
    return pl.ds(pl.multiple_of(step * LANES, LANES), LANES)


def head_products(mine, other, part, here, into):
    for h, rows in enumerate(head_slices(mine.shape[1])):
        left = mine[part, rows, here].astype(jnp.float32)
        for slot, get in enumerate(other):
            product = left * get(part, rows).astype(jnp.float32)
            into[slot, h * SUBLANES:(h + 1) * SUBLANES, :] = jnp.sum(product.reshape(-1, SUBLANES, LANES), axis=0)


def sublane_total(ref, slot):
    parts = [ref[slot, pl.ds(i, HEADS, stride=SUBLANES), :] for i in range(SUBLANES)]
    while len(parts) > 1:
        parts = [a + b for a, b in zip(parts[::2], parts[1::2])]
    return parts[0]


def product_kernel(n_two, n_one, n_other, qg, *rest):
    *sources, out, work = rest
    others = sources[:n_other]
    two, one = sources[n_other:n_other + n_two], sources[n_other + n_two:]

    @pl.loop(0, qg.shape[2] // LANES)
    def _(step):
        here = lanes(step)
        getters = [choose([o], 0, 1, here) for o in others]
        getters += [choose(blocks, bit, 1, here) for blocks, bit in ((one, 0), (two, 1)) if blocks]
        for part in range(2):
            head_products(qg, getters, part, here, work)
            for slot in range(len(getters)):
                out[part, slot, :, here] = sublane_total(work, slot)


def products_of(qg, others, two, one, weight):
    rows = qg.shape[2]
    slots = len(others) + bool(two) + bool(one)
    return pl.pallas_call(
        functools.partial(product_kernel, len(two), len(one), len(others)),
        in_specs=[VMEM] * (1 + len(others) + len(two) + len(one)),
        out_specs=VMEM,
        out_shape=jax.ShapeDtypeStruct((2, slots, HEADS, rows), jnp.float32),
        scratch_shapes=[pltpu.VMEM((slots, HEADS * SUBLANES, LANES), jnp.float32)],
        compiler_params=params(),
        cost_estimate=pl.CostEstimate(flops=int(weight * US_FLOPS), bytes_accessed=int(weight * US), transcendentals=0),
        name="products",
    )(qg, *others, *two, *one)


def score_kernel(head_size, links, near0, near1, far0, far1, self_pair, pair1, pair2, pair4, pair8):
    scale = head_size ** (-0.5)
    half = far0.shape[-1]
    for start, near, far in ((0, near0, far0), (half, near1, far1)):
        here = slice(start, start + half)
        products = [[near[part, 0], near[part, 2], near[part, 3], near[part, 1], far[part, 0]] for part in range(2)]
        scores = [p * scale for p in products[0]]
        scores = scores[:1] + [jnp.where(links[0, j] > 0, s, -1e30) for j, s in enumerate(scores[1:])]
        highest = functools.reduce(jnp.maximum, scores)
        raw = [jnp.exp(s - highest) for s in scores]
        raw = raw[:1] + [jnp.where(links[0, j] > 0, r, 0.0) for j, r in enumerate(raw[1:])]
        total = functools.reduce(jnp.add, raw)
        probability = [r / total for r in raw]
        inner = functools.reduce(jnp.add, [p * g for p, g in zip(probability, products[1])])
        for pair, p, g in zip((self_pair, pair1, pair2, pair4, pair8), probability, products[1]):
            pair[:HEADS, here] = p * (g - inner) * scale
            pair[HEADS:, here] = p


def scores_of(links, near0, near1, far0, far1, head_size, weight):
    pair = jax.ShapeDtypeStruct((2 * HEADS, 2 * far0.shape[-1]), jnp.float32)
    return pl.pallas_call(
        functools.partial(score_kernel, head_size),
        in_specs=[SMEM] + [VMEM] * 4,
        out_specs=[VMEM] * 5,
        out_shape=[pair] * 5,
        compiler_params=params(),
        cost_estimate=pl.CostEstimate(flops=int(weight * US_FLOPS), bytes_accessed=int(weight * US), transcendentals=0),
        name="scores",
    )(links, near0, near1, far0, far1)


def query_kernel(start, own, two_a, two_b, one_a, one_b, far4, far8, self_pair, pair1, pair2, pair4, pair8, w_query, out,
                 grad_query):
    _, width, patches = own.shape
    pairs = (self_pair, pair1, pair2, pair4, pair8)

    @pl.loop(0, patches // LANES)
    def _(step):
        here = lanes(step)
        there = lanes(step + start // LANES)
        getters = source_getters(own, (two_a, two_b), (one_a, one_b), far4, far8, 1, here)
        for h, rows in enumerate(head_slices(width)):
            terms = [pairs[s][h:h + 1, there] * get(0, rows).astype(jnp.float32) for s, get in enumerate(getters)]
            grad_query[rows, here] = functools.reduce(jnp.add, terms).astype(jnp.bfloat16)

    out[...] = jnp.dot(w_query[...], grad_query[...], preferred_element_type=jnp.float32)


def query_part_of(own, two, one, far4, far8, pairs, w_query, start, weight):
    _, width, rows = own.shape
    return pl.pallas_call(
        functools.partial(query_kernel, start),
        in_specs=[VMEM] * 13,
        out_specs=VMEM,
        out_shape=jax.ShapeDtypeStruct((w_query.shape[0], rows), jnp.float32),
        scratch_shapes=[pltpu.VMEM((width, rows), jnp.bfloat16)],
        compiler_params=params(),
        cost_estimate=pl.CostEstimate(flops=int(weight * US_FLOPS), bytes_accessed=int(weight * US), transcendentals=0),
        name="query_part",
    )(own, *two, *one, far4, far8, *pairs, w_query)


def sum_kernel(shapes, self_pair, pair8, pair4, pair2, pair1, w_key, w_value, *rest):
    out, key_ref, value_ref, result, sems = rest[-5:]
    rest = rest[:-5]
    pairs = (self_pair, pair1, pair2, pair4, pair8)
    copies = []
    for i, (n_two, n_one) in enumerate(shapes):
        own, query_part, far4, far8 = rest[:4]
        two, one, rest = rest[4:4 + n_two], rest[4 + n_two:4 + n_two + n_one], rest[4 + n_two + n_one:]
        _, width, patches = own.shape

        @pl.loop(0, patches // LANES)
        def _(step):
            here = lanes(step)
            there = lanes(step + i * (patches // LANES))
            getters = source_getters(own, two, one, far4, far8, 0, here)
            for h, rows in enumerate(head_slices(width)):
                for part, into in ((0, key_ref), (1, value_ref)):
                    row = part * HEADS + h
                    terms = [pairs[s][row:row + 1, there] * get(part, rows).astype(jnp.float32)
                             for s, get in enumerate(getters)]
                    into[rows, there] = functools.reduce(jnp.add, terms).astype(jnp.bfloat16)

        columns = pl.ds(i * patches, patches)
        for o in range(0, width, PIECE):
            piece = slice(o, o + PIECE)
            total = query_part[piece, :] + jnp.dot(
                w_key[piece, :], key_ref[:, columns], preferred_element_type=jnp.float32)
            total = total + jnp.dot(w_value[piece, :], value_ref[:, columns], preferred_element_type=jnp.float32)
            result[columns, piece] = total.astype(jnp.bfloat16).T
        copies.append(pltpu.make_async_copy(result.at[columns, :], out.at[columns, :], sems.at[i]))
        copies[-1].start()
    for copy in copies:
        copy.wait()


def sums_of(halves, pairs, weights, weight):
    _, width, rows = halves[0][0].shape
    operands = [*pairs, *weights]
    for own, query_part, two, one, far4, far8 in halves:
        operands += [own, query_part, far4, far8, *two, *one]
    return pl.pallas_call(
        functools.partial(sum_kernel, [(len(h[2]), len(h[3])) for h in halves]),
        in_specs=[VMEM] * len(operands),
        out_specs=pl.BlockSpec(memory_space=pl.ANY),
        out_shape=jax.ShapeDtypeStruct((2 * rows, width), jnp.bfloat16),
        scratch_shapes=[pltpu.VMEM((width, 2 * rows), jnp.bfloat16)] * 2
        + [pltpu.VMEM((2 * rows, width), jnp.bfloat16), pltpu.SemaphoreType.DMA((2,))],
        compiler_params=params(),
        cost_estimate=pl.CostEstimate(flops=int(weight * US_FLOPS), bytes_accessed=int(weight * US), transcendentals=0),
        name="sums",
    )(*operands)


def per_device(queries, keys, values, grad_out, links, w_query, w_key, w_value):
    patches = queries.shape[1]
    half = patches // 2
    head_size = keys.shape[2] // HEADS
    kv0, qg0, owed = pack(queries, keys, values, grad_out, 0, half, True)
    kv1, qg1 = pack(after(queries, kv0), keys, values, grad_out, half, half, False)
    up4_0 = shift(kv0, 4)
    down4_0 = shift(qg0, -4)
    y_a = swap(owed, 2)
    up4_1 = shift(kv1, 4)
    down4_1 = shift(qg1, -4)
    y_b = swap(after(pick((kv1, up4_0), BY_BIT1, 0), y_a, down4_0), 2)
    up8_0 = shift(after(up4_0, down4_0), 4)
    down8_0 = shift(after(down4_0, up4_0), -4)
    c_a = swap(pick((after(kv0, up4_1, down4_1), qg0), BY_BIT0, 2.8), 1)
    y_c = swap(pick((down4_0, up4_1), BY_BIT1, 3), 2)
    up8_1 = shift(after(up4_1, y_b), 4)
    down8_1 = shift(after(down4_1, up8_0, down8_0), -4)
    c_b = swap(pick((kv1, y_b, y_a), (0, 1, 0, 2), 0), 1)
    near0 = products_of(qg0, [kv0, up4_0], (y_a, y_b), (c_a, c_b), 4)
    far0 = products_of(after(qg0, down8_0), [up8_0], (), (), 5.7)
    c_c = swap(after(pick((y_a, y_c, y_b), (0, 1, 1, 2), 0), near0, far0), 1)
    near1 = products_of(qg1, [kv1, up4_1], (y_b, y_c), (c_b, c_c), 0)
    y_d = swap(after(pick((down4_1, qg1), BY_BIT1, 0), up8_0, down8_0), 2)
    far1 = products_of(after(qg1, c_b), [up8_1], (), (), 10)
    pairs = scores_of(links, after(near0, down8_0), near1, far0, far1, head_size, 0)
    self_pair, pair1, pair2, pair4, pair8 = pairs
    came8 = shift(pair8, -8)
    came4 = shift(pair4, -4)
    came2 = shift(pair2, -2)
    came1 = shift(pair1, -1)
    query_part0 = query_part_of(kv0, (y_a, y_b), (c_a, c_b), up4_0, up8_0, pairs, w_query, 0, 0)
    query_part1 = query_part_of(kv1, (y_b, y_c), (c_b, c_c), up4_1, up8_1, pairs, w_query, half, 0)
    c_d = swap(pick((y_d, qg1), BY_BIT0, 0), 1)
    halves = (
        (qg0, query_part0, (y_a, y_c), (c_a, c_c), down4_0, down8_0),
        (qg1, query_part1, (y_d,), (c_d,), down4_1, down8_1),
    )
    out = sums_of(halves, (self_pair, came8, came4, came2, came1), (w_key, w_value), 3)
    return out[None]


def solution(mesh):
    by_frame = P(("dom", "frame"), None, None)
    return jax.shard_map(
        per_device,
        mesh=mesh,
        in_specs=(by_frame,) * 4 + (P(("dom", "frame"), None), P(), P(), P()),
        out_specs=by_frame,
        check_vma=False,
    )
```

```python
import functools

import jax
import jax.numpy as jnp
from jax import lax
from jax.experimental import pallas as pl
from jax.experimental.pallas import tpu as pltpu
from jax.sharding import PartitionSpec as P

HEADS = 16
NDIL = 4
LANES = 128
SUBLANES = 8
PIECE = 256
US = 3.69e6
US_FLOPS = 1.15e9
BY_BIT0, BY_BIT1 = (0, 1, 0, 1), (0, 0, 1, 1)
VMEM_BYTES = 32 * 2**20


def shift(block, distance):
    n = lax.axis_size("frame")
    return lax.ppermute(block, "frame", [(i, i + distance) for i in range(n) if 0 <= i + distance < n])


def swap(block, bit):
    n = lax.axis_size("frame")
    return lax.ppermute(block, "frame", [(i, i ^ bit) for i in range(n)])


def place_bit(bit):
    return lax.rem(lax.axis_index("frame") // 2**bit, 2)


def params():
    return pltpu.CompilerParams(vmem_limit_bytes=VMEM_BYTES)


SMEM = pl.BlockSpec(memory_space=pltpu.SMEM)
VMEM = pl.BlockSpec(memory_space=pltpu.VMEM)


def after(block, *done):
    return lax.optimization_barrier((block, *done))[0] if done else block


def pack(queries, keys, values, grad_out, start, rows, with_owed):
    width = queries.shape[2]

    def kernel(q_hbm, k_hbm, v_hbm, g_hbm, kv_out, qg_out, *rest):
        owed, (q_ref, k_ref, v_ref, g_ref, sems) = rest[:-5], rest[-5:]
        pieces = []
        for part, up, down in ((0, (k_hbm, k_ref), (q_hbm, q_ref)), (1, (v_hbm, v_ref), (g_hbm, g_ref))):
            for (hbm, ref), out, bit in ((up, kv_out, 0), (down, qg_out, 1)):
                copy = pltpu.make_async_copy(hbm.at[0, pl.ds(start, rows), :], ref, sems.at[len(pieces)])
                pieces.append((copy, ref, out, part, bit))
        for piece in pieces:
            piece[0].start()
        for copy, ref, out, part, bit in pieces:
            copy.wait()
            for p in range(0, rows, LANES):
                turned = ref[p:p + LANES, :].T
                out[part, :, p:p + LANES] = turned
                for y_out in owed:
                    @pl.when(place_bit(1) == bit)
                    def _():
                        y_out[part, :, p:p + LANES] = turned

    shape = jax.ShapeDtypeStruct((2, width, rows), jnp.bfloat16)
    n_out = 3 if with_owed else 2
    return pl.pallas_call(
        kernel,
        in_specs=[pl.BlockSpec(memory_space=pl.ANY)] * 4,
        out_specs=[VMEM] * n_out,
        out_shape=[shape] * n_out,
        scratch_shapes=[pltpu.VMEM((rows, width), jnp.bfloat16)] * 4 + [pltpu.SemaphoreType.DMA((4,))],
        compiler_params=params(),
        name="pack",
    )(*(pltpu.with_memory_space_constraint(a, pltpu.HBM) for a in (queries, keys, values, grad_out)))


def pick(blocks, which, weight=1):
    def kernel(*refs):
        place = 2 * place_bit(1) + place_bit(0)
        for number, ref in enumerate(refs[:-1]):
            mine = [place == p for p in range(4) if which[p] == number]

            @pl.when(functools.reduce(jnp.logical_or, mine))
            def _(ref=ref):
                refs[-1][...] = ref[...]

    size = blocks[0].size
    return pl.pallas_call(
        kernel,
        in_specs=[VMEM] * len(blocks),
        out_specs=VMEM,
        out_shape=jax.ShapeDtypeStruct(blocks[0].shape, blocks[0].dtype),
        compiler_params=params(),
        cost_estimate=pl.CostEstimate(flops=int(weight * US_FLOPS), bytes_accessed=int(weight * US), transcendentals=0),
        name="pick",
    )(*blocks)


def choose(blocks, bit, wanted, here):
    if len(blocks) == 1:
        return lambda i, rows: blocks[0][i, rows, here]
    use_first = place_bit(bit) == wanted
    return lambda i, rows: jnp.where(use_first, blocks[0][i, rows, here], blocks[1][i, rows, here])


def source_getters(own, two, one, far4, far8, wanted, here):
    return (
        choose([own], 0, wanted, here),
        choose(one, 0, wanted, here),
        choose(two, 1, wanted, here),
        choose([far4], 0, wanted, here),
        choose([far8], 0, wanted, here),
    )


def head_slices(width):
    size = width // HEADS
    return [slice(h * size, (h + 1) * size) for h in range(HEADS)]


def lanes(step):
    return pl.ds(pl.multiple_of(step * LANES, LANES), LANES)


def head_products(mine, other, part, here, into):
    for h, rows in enumerate(head_slices(mine.shape[1])):
        left = mine[part, rows, here].astype(jnp.float32)
        for slot, get in enumerate(other):
            product = left * get(part, rows).astype(jnp.float32)
            into[slot, h * SUBLANES:(h + 1) * SUBLANES, :] = jnp.sum(product.reshape(-1, SUBLANES, LANES), axis=0)


def sublane_total(ref, slot):
    parts = [ref[slot, pl.ds(i, HEADS, stride=SUBLANES), :] for i in range(SUBLANES)]
    while len(parts) > 1:
        parts = [a + b for a, b in zip(parts[::2], parts[1::2])]
    return parts[0]


def product_kernel(n_two, n_one, n_other, qg, *rest):
    *sources, out, work = rest
    others = sources[:n_other]
    two, one = sources[n_other:n_other + n_two], sources[n_other + n_two:]

    @pl.loop(0, qg.shape[2] // LANES)
    def _(step):
        here = lanes(step)
        getters = [choose([o], 0, 1, here) for o in others]
        getters += [choose(blocks, bit, 1, here) for blocks, bit in ((one, 0), (two, 1)) if blocks]
        for part in range(2):
            head_products(qg, getters, part, here, work)
            for slot in range(len(getters)):
                out[part, slot, :, here] = sublane_total(work, slot)


def products_of(qg, others, two, one, weight):
    rows = qg.shape[2]
    slots = len(others) + bool(two) + bool(one)
    return pl.pallas_call(
        functools.partial(product_kernel, len(two), len(one), len(others)),
        in_specs=[VMEM] * (1 + len(others) + len(two) + len(one)),
        out_specs=VMEM,
        out_shape=jax.ShapeDtypeStruct((2, slots, HEADS, rows), jnp.float32),
        scratch_shapes=[pltpu.VMEM((slots, HEADS * SUBLANES, LANES), jnp.float32)],
        compiler_params=params(),
        cost_estimate=pl.CostEstimate(flops=int(weight * US_FLOPS), bytes_accessed=int(weight * US), transcendentals=0),
        name="products",
    )(qg, *others, *two, *one)


def score_kernel(head_size, links, near0, near1, far0, far1, self_pair, pair1, pair2, pair4, pair8):
    scale = head_size ** (-0.5)
    half = far0.shape[-1]
    for start, near, far in ((0, near0, far0), (half, near1, far1)):
        here = slice(start, start + half)
        products = [[near[part, 0], near[part, 2], near[part, 3], near[part, 1], far[part, 0]] for part in range(2)]
        scores = [p * scale for p in products[0]]
        scores = scores[:1] + [jnp.where(links[0, j] > 0, s, -1e30) for j, s in enumerate(scores[1:])]
        highest = functools.reduce(jnp.maximum, scores)
        raw = [jnp.exp(s - highest) for s in scores]
        raw = raw[:1] + [jnp.where(links[0, j] > 0, r, 0.0) for j, r in enumerate(raw[1:])]
        total = functools.reduce(jnp.add, raw)
        probability = [r / total for r in raw]
        inner = functools.reduce(jnp.add, [p * g for p, g in zip(probability, products[1])])
        for pair, p, g in zip((self_pair, pair1, pair2, pair4, pair8), probability, products[1]):
            pair[:HEADS, here] = p * (g - inner) * scale
            pair[HEADS:, here] = p


def scores_of(links, near0, near1, far0, far1, head_size, weight):
    pair = jax.ShapeDtypeStruct((2 * HEADS, 2 * far0.shape[-1]), jnp.float32)
    return pl.pallas_call(
        functools.partial(score_kernel, head_size),
        in_specs=[SMEM] + [VMEM] * 4,
        out_specs=[VMEM] * 5,
        out_shape=[pair] * 5,
        compiler_params=params(),
        cost_estimate=pl.CostEstimate(flops=int(weight * US_FLOPS), bytes_accessed=int(weight * US), transcendentals=0),
        name="scores",
    )(links, near0, near1, far0, far1)


def query_kernel(start, own, two_a, two_b, one_a, one_b, far4, far8, self_pair, pair1, pair2, pair4, pair8, w_query, out,
                 grad_query):
    _, width, patches = own.shape
    pairs = (self_pair, pair1, pair2, pair4, pair8)

    @pl.loop(0, patches // LANES)
    def _(step):
        here = lanes(step)
        there = lanes(step + start // LANES)
        getters = source_getters(own, (two_a, two_b), (one_a, one_b), far4, far8, 1, here)
        for h, rows in enumerate(head_slices(width)):
            terms = [pairs[s][h:h + 1, there] * get(0, rows).astype(jnp.float32) for s, get in enumerate(getters)]
            grad_query[rows, here] = functools.reduce(jnp.add, terms).astype(jnp.bfloat16)

    out[...] = jnp.dot(w_query[...], grad_query[...], preferred_element_type=jnp.float32)


def query_part_of(own, two, one, far4, far8, pairs, w_query, start, weight):
    _, width, rows = own.shape
    return pl.pallas_call(
        functools.partial(query_kernel, start),
        in_specs=[VMEM] * 13,
        out_specs=VMEM,
        out_shape=jax.ShapeDtypeStruct((w_query.shape[0], rows), jnp.float32),
        scratch_shapes=[pltpu.VMEM((width, rows), jnp.bfloat16)],
        compiler_params=params(),
        cost_estimate=pl.CostEstimate(flops=int(weight * US_FLOPS), bytes_accessed=int(weight * US), transcendentals=0),
        name="query_part",
    )(own, *two, *one, far4, far8, *pairs, w_query)


def sum_kernel(shapes, self_pair, pair8, pair4, pair2, pair1, w_key, w_value, *rest):
    out, key_ref, value_ref, result, sems = rest[-5:]
    rest = rest[:-5]
    pairs = (self_pair, pair1, pair2, pair4, pair8)
    copies = []
    for i, (n_two, n_one) in enumerate(shapes):
        own, query_part, far4, far8 = rest[:4]
        two, one, rest = rest[4:4 + n_two], rest[4 + n_two:4 + n_two + n_one], rest[4 + n_two + n_one:]
        _, width, patches = own.shape

        for step in range(patches // LANES):
            here = slice(step * LANES, (step + 1) * LANES)
            there = slice(i * patches + step * LANES, i * patches + (step + 1) * LANES)
            getters = source_getters(own, two, one, far4, far8, 0, here)
            for h, rows in enumerate(head_slices(width)):
                for part, into in ((0, key_ref), (1, value_ref)):
                    row = part * HEADS + h
                    terms = [pairs[s][row:row + 1, there] * get(part, rows).astype(jnp.float32)
                             for s, get in enumerate(getters)]
                    into[rows, there] = functools.reduce(jnp.add, terms).astype(jnp.bfloat16)

        columns = slice(i * patches, (i + 1) * patches)
        for o in range(0, width, PIECE):
            piece = slice(o, o + PIECE)
            total = query_part[piece, :] + jnp.dot(
                w_key[piece, :], key_ref[:, columns], preferred_element_type=jnp.float32)
            total = total + jnp.dot(w_value[piece, :], value_ref[:, columns], preferred_element_type=jnp.float32)
            result[columns, piece] = total.astype(jnp.bfloat16).T
        copies.append(pltpu.make_async_copy(result.at[columns, :], out.at[columns, :], sems.at[i]))
        copies[-1].start()
    for copy in copies:
        copy.wait()


def sums_of(halves, pairs, weights, weight):
    _, width, rows = halves[0][0].shape
    operands = [*pairs, *weights]
    for own, query_part, two, one, far4, far8 in halves:
        operands += [own, query_part, far4, far8, *two, *one]
    return pl.pallas_call(
        functools.partial(sum_kernel, [(len(h[2]), len(h[3])) for h in halves]),
        in_specs=[VMEM] * len(operands),
        out_specs=pl.BlockSpec(memory_space=pl.ANY),
        out_shape=jax.ShapeDtypeStruct((2 * rows, width), jnp.bfloat16),
        scratch_shapes=[pltpu.VMEM((width, 2 * rows), jnp.bfloat16)] * 2
        + [pltpu.VMEM((2 * rows, width), jnp.bfloat16), pltpu.SemaphoreType.DMA((2,))],
        compiler_params=params(),
        cost_estimate=pl.CostEstimate(flops=int(weight * US_FLOPS), bytes_accessed=int(weight * US), transcendentals=0),
        name="sums",
    )(*operands)


def per_device(queries, keys, values, grad_out, links, w_query, w_key, w_value):
    patches = queries.shape[1]
    half = patches // 2
    head_size = keys.shape[2] // HEADS
    kv0, qg0, owed = pack(queries, keys, values, grad_out, 0, half, True)
    kv1, qg1 = pack(after(queries, kv0), keys, values, grad_out, half, half, False)
    up4_0 = shift(kv0, 4)
    down4_0 = shift(qg0, -4)
    y_a = swap(owed, 2)
    up4_1 = shift(kv1, 4)
    down4_1 = shift(qg1, -4)
    y_b = swap(after(pick((kv1, up4_0), BY_BIT1, 0), y_a, down4_0), 2)
    up8_0 = shift(after(up4_0, down4_0), 4)
    down8_0 = shift(after(down4_0, up4_0), -4)
    c_a = swap(pick((after(kv0, up4_1, down4_1), qg0), BY_BIT0, 2.8), 1)
    y_c = swap(pick((down4_0, up4_1), BY_BIT1, 3), 2)
    up8_1 = shift(after(up4_1, y_b), 4)
    down8_1 = shift(after(down4_1, up8_0, down8_0), -4)
    c_b = swap(pick((kv1, y_b, y_a), (0, 1, 0, 2), 0), 1)
    near0 = products_of(qg0, [kv0, up4_0], (y_a, y_b), (c_a, c_b), 4)
    far0 = products_of(after(qg0, down8_0), [up8_0], (), (), 5.7)
    c_c = swap(after(pick((y_a, y_c, y_b), (0, 1, 1, 2), 0), near0, far0), 1)
    near1 = products_of(qg1, [kv1, up4_1], (y_b, y_c), (c_b, c_c), 0)
    y_d = swap(after(pick((down4_1, qg1), BY_BIT1, 0), up8_0, down8_0), 2)
    far1 = products_of(after(qg1, c_b), [up8_1], (), (), 10)
    pairs = scores_of(links, after(near0, down8_0), near1, far0, far1, head_size, 0)
    self_pair, pair1, pair2, pair4, pair8 = pairs
    came8 = shift(pair8, -8)
    came4 = shift(pair4, -4)
    came2 = shift(pair2, -2)
    came1 = shift(pair1, -1)
    query_part0 = query_part_of(kv0, (y_a, y_b), (c_a, c_b), up4_0, up8_0, pairs, w_query, 0, 0)
    query_part1 = query_part_of(kv1, (y_b, y_c), (c_b, c_c), up4_1, up8_1, pairs, w_query, half, 0)
    c_d = swap(pick((y_d, qg1), BY_BIT0, 0), 1)
    halves = (
        (qg0, query_part0, (y_a, y_c), (c_a, c_c), down4_0, down8_0),
        (qg1, query_part1, (y_d,), (c_d,), down4_1, down8_1),
    )
    out = sums_of(halves, (self_pair, came8, came4, came2, came1), (w_key, w_value), 3)
    return out[None]


def solution(mesh):
    by_frame = P(("dom", "frame"), None, None)
    return jax.shard_map(
        per_device,
        mesh=mesh,
        in_specs=(by_frame,) * 4 + (P(("dom", "frame"), None), P(), P(), P()),
        out_specs=by_frame,
        check_vma=False,
    )
```

```python
import functools

import jax
import jax.numpy as jnp
from jax import lax
from jax.experimental import pallas as pl
from jax.experimental.pallas import tpu as pltpu
from jax.sharding import PartitionSpec as P

HEADS = 16
NDIL = 4
LANES = 128
SUBLANES = 8
PIECE = 256
US = 3.69e6
US_FLOPS = 1.15e9
BY_BIT0, BY_BIT1 = (0, 1, 0, 1), (0, 0, 1, 1)
VMEM_BYTES = 32 * 2**20


def shift(block, distance):
    n = lax.axis_size("frame")
    return lax.ppermute(block, "frame", [(i, i + distance) for i in range(n) if 0 <= i + distance < n])


def swap(block, bit):
    n = lax.axis_size("frame")
    return lax.ppermute(block, "frame", [(i, i ^ bit) for i in range(n)])


def place_bit(bit):
    return lax.rem(lax.axis_index("frame") // 2**bit, 2)


def params():
    return pltpu.CompilerParams(vmem_limit_bytes=VMEM_BYTES)


SMEM = pl.BlockSpec(memory_space=pltpu.SMEM)
VMEM = pl.BlockSpec(memory_space=pltpu.VMEM)


def after(block, *done):
    return lax.optimization_barrier((block, *done))[0] if done else block


def pack(queries, keys, values, grad_out, start, rows, with_owed):
    width = queries.shape[2]

    def kernel(q_hbm, k_hbm, v_hbm, g_hbm, kv_out, qg_out, *rest):
        owed, (q_ref, k_ref, v_ref, g_ref, sems) = rest[:-5], rest[-5:]
        pieces = []
        for part, up, down in ((0, (k_hbm, k_ref), (q_hbm, q_ref)), (1, (v_hbm, v_ref), (g_hbm, g_ref))):
            for (hbm, ref), out, bit in ((up, kv_out, 0), (down, qg_out, 1)):
                copy = pltpu.make_async_copy(hbm.at[0, pl.ds(start, rows), :], ref, sems.at[len(pieces)])
                pieces.append((copy, ref, out, part, bit))
        for piece in pieces:
            piece[0].start()
        for copy, ref, out, part, bit in pieces:
            copy.wait()
            for p in range(0, rows, LANES):
                turned = ref[p:p + LANES, :].T
                out[part, :, p:p + LANES] = turned
                for y_out in owed:
                    @pl.when(place_bit(1) == bit)
                    def _():
                        y_out[part, :, p:p + LANES] = turned

    shape = jax.ShapeDtypeStruct((2, width, rows), jnp.bfloat16)
    n_out = 3 if with_owed else 2
    return pl.pallas_call(
        kernel,
        in_specs=[pl.BlockSpec(memory_space=pl.ANY)] * 4,
        out_specs=[VMEM] * n_out,
        out_shape=[shape] * n_out,
        scratch_shapes=[pltpu.VMEM((rows, width), jnp.bfloat16)] * 4 + [pltpu.SemaphoreType.DMA((4,))],
        compiler_params=params(),
        name="pack",
    )(*(pltpu.with_memory_space_constraint(a, pltpu.HBM) for a in (queries, keys, values, grad_out)))


def pick(blocks, which, weight=1):
    def kernel(*refs):
        place = 2 * place_bit(1) + place_bit(0)
        for number, ref in enumerate(refs[:-1]):
            mine = [place == p for p in range(4) if which[p] == number]

            @pl.when(functools.reduce(jnp.logical_or, mine))
            def _(ref=ref):
                refs[-1][...] = ref[...]

    size = blocks[0].size
    return pl.pallas_call(
        kernel,
        in_specs=[VMEM] * len(blocks),
        out_specs=VMEM,
        out_shape=jax.ShapeDtypeStruct(blocks[0].shape, blocks[0].dtype),
        compiler_params=params(),
        cost_estimate=pl.CostEstimate(flops=int(weight * US_FLOPS), bytes_accessed=int(weight * US), transcendentals=0),
        name="pick",
    )(*blocks)


def choose(blocks, bit, wanted, here):
    if len(blocks) == 1:
        return lambda i, rows: blocks[0][i, rows, here]
    use_first = place_bit(bit) == wanted
    return lambda i, rows: jnp.where(use_first, blocks[0][i, rows, here], blocks[1][i, rows, here])


def source_getters(own, two, one, far4, far8, wanted, here):
    return (
        choose([own], 0, wanted, here),
        choose(one, 0, wanted, here),
        choose(two, 1, wanted, here),
        choose([far4], 0, wanted, here),
        choose([far8], 0, wanted, here),
    )


def head_slices(width):
    size = width // HEADS
    return [slice(h * size, (h + 1) * size) for h in range(HEADS)]


def lanes(step):
    return pl.ds(pl.multiple_of(step * LANES, LANES), LANES)


def head_products(mine, other, part, here, into):
    for h, rows in enumerate(head_slices(mine.shape[1])):
        left = mine[part, rows, here].astype(jnp.float32)
        for slot, get in enumerate(other):
            product = left * get(part, rows).astype(jnp.float32)
            into[slot, h * SUBLANES:(h + 1) * SUBLANES, :] = jnp.sum(product.reshape(-1, SUBLANES, LANES), axis=0)


def sublane_total(ref, slot):
    parts = [ref[slot, pl.ds(i, HEADS, stride=SUBLANES), :] for i in range(SUBLANES)]
    while len(parts) > 1:
        parts = [a + b for a, b in zip(parts[::2], parts[1::2])]
    return parts[0]


def product_kernel(n_two, n_one, n_other, qg, *rest):
    *sources, out, work = rest
    others = sources[:n_other]
    two, one = sources[n_other:n_other + n_two], sources[n_other + n_two:]

    @pl.loop(0, qg.shape[2] // LANES)
    def _(step):
        here = lanes(step)
        getters = [choose([o], 0, 1, here) for o in others]
        getters += [choose(blocks, bit, 1, here) for blocks, bit in ((one, 0), (two, 1)) if blocks]
        for part in range(2):
            head_products(qg, getters, part, here, work)
            for slot in range(len(getters)):
                out[part, slot, :, here] = sublane_total(work, slot)


def products_of(qg, others, two, one, weight):
    rows = qg.shape[2]
    slots = len(others) + bool(two) + bool(one)
    return pl.pallas_call(
        functools.partial(product_kernel, len(two), len(one), len(others)),
        in_specs=[VMEM] * (1 + len(others) + len(two) + len(one)),
        out_specs=VMEM,
        out_shape=jax.ShapeDtypeStruct((2, slots, HEADS, rows), jnp.float32),
        scratch_shapes=[pltpu.VMEM((slots, HEADS * SUBLANES, LANES), jnp.float32)],
        compiler_params=params(),
        cost_estimate=pl.CostEstimate(flops=int(weight * US_FLOPS), bytes_accessed=int(weight * US), transcendentals=0),
        name="products",
    )(qg, *others, *two, *one)


def score_kernel(head_size, links, near0, near1, far0, far1, self_pair, pair1, pair2, pair4, pair8):
    scale = head_size ** (-0.5)
    half = far0.shape[-1]
    for start, near, far in ((0, near0, far0), (half, near1, far1)):
        here = slice(start, start + half)
        products = [[near[part, 0], near[part, 2], near[part, 3], near[part, 1], far[part, 0]] for part in range(2)]
        scores = [p * scale for p in products[0]]
        scores = scores[:1] + [jnp.where(links[0, j] > 0, s, -1e30) for j, s in enumerate(scores[1:])]
        highest = functools.reduce(jnp.maximum, scores)
        raw = [jnp.exp(s - highest) for s in scores]
        raw = raw[:1] + [jnp.where(links[0, j] > 0, r, 0.0) for j, r in enumerate(raw[1:])]
        total = functools.reduce(jnp.add, raw)
        probability = [r / total for r in raw]
        inner = functools.reduce(jnp.add, [p * g for p, g in zip(probability, products[1])])
        for pair, p, g in zip((self_pair, pair1, pair2, pair4, pair8), probability, products[1]):
            pair[:HEADS, here] = p * (g - inner) * scale
            pair[HEADS:, here] = p


def scores_of(links, near0, near1, far0, far1, head_size, weight):
    pair = jax.ShapeDtypeStruct((2 * HEADS, 2 * far0.shape[-1]), jnp.float32)
    return pl.pallas_call(
        functools.partial(score_kernel, head_size),
        in_specs=[SMEM] + [VMEM] * 4,
        out_specs=[VMEM] * 5,
        out_shape=[pair] * 5,
        compiler_params=params(),
        cost_estimate=pl.CostEstimate(flops=int(weight * US_FLOPS), bytes_accessed=int(weight * US), transcendentals=0),
        name="scores",
    )(links, near0, near1, far0, far1)


def query_kernel(start, own, two_a, two_b, one_a, one_b, far4, far8, self_pair, pair1, pair2, pair4, pair8, w_query, out,
                 grad_query):
    _, width, patches = own.shape
    pairs = (self_pair, pair1, pair2, pair4, pair8)

    for step in range(patches // LANES):
        here = slice(step * LANES, (step + 1) * LANES)
        there = slice(start + step * LANES, start + (step + 1) * LANES)
        getters = source_getters(own, (two_a, two_b), (one_a, one_b), far4, far8, 1, here)
        for h, rows in enumerate(head_slices(width)):
            terms = [pairs[s][h:h + 1, there] * get(0, rows).astype(jnp.float32) for s, get in enumerate(getters)]
            grad_query[rows, here] = functools.reduce(jnp.add, terms).astype(jnp.bfloat16)

    out[...] = jnp.dot(w_query[...], grad_query[...], preferred_element_type=jnp.float32)


def query_part_of(own, two, one, far4, far8, pairs, w_query, start, weight):
    _, width, rows = own.shape
    return pl.pallas_call(
        functools.partial(query_kernel, start),
        in_specs=[VMEM] * 13,
        out_specs=VMEM,
        out_shape=jax.ShapeDtypeStruct((w_query.shape[0], rows), jnp.float32),
        scratch_shapes=[pltpu.VMEM((width, rows), jnp.bfloat16)],
        compiler_params=params(),
        cost_estimate=pl.CostEstimate(flops=int(weight * US_FLOPS), bytes_accessed=int(weight * US), transcendentals=0),
        name="query_part",
    )(own, *two, *one, far4, far8, *pairs, w_query)


def sum_kernel(shapes, self_pair, pair8, pair4, pair2, pair1, w_key, w_value, *rest):
    out, key_ref, value_ref, result, sems = rest[-5:]
    rest = rest[:-5]
    pairs = (self_pair, pair1, pair2, pair4, pair8)
    copies = []
    for i, (n_two, n_one) in enumerate(shapes):
        own, query_part, far4, far8 = rest[:4]
        two, one, rest = rest[4:4 + n_two], rest[4 + n_two:4 + n_two + n_one], rest[4 + n_two + n_one:]
        _, width, patches = own.shape

        for step in range(patches // LANES):
            here = slice(step * LANES, (step + 1) * LANES)
            there = slice(i * patches + step * LANES, i * patches + (step + 1) * LANES)
            getters = source_getters(own, two, one, far4, far8, 0, here)
            for h, rows in enumerate(head_slices(width)):
                for part, into in ((0, key_ref), (1, value_ref)):
                    row = part * HEADS + h
                    terms = [pairs[s][row:row + 1, there] * get(part, rows).astype(jnp.float32)
                             for s, get in enumerate(getters)]
                    into[rows, there] = functools.reduce(jnp.add, terms).astype(jnp.bfloat16)

        columns = slice(i * patches, (i + 1) * patches)
        for o in range(0, width, PIECE):
            piece = slice(o, o + PIECE)
            total = query_part[piece, :] + jnp.dot(
                w_key[piece, :], key_ref[:, columns], preferred_element_type=jnp.float32)
            total = total + jnp.dot(w_value[piece, :], value_ref[:, columns], preferred_element_type=jnp.float32)
            result[columns, piece] = total.astype(jnp.bfloat16).T
        copies.append(pltpu.make_async_copy(result.at[columns, :], out.at[columns, :], sems.at[i]))
        copies[-1].start()
    for copy in copies:
        copy.wait()


def sums_of(halves, pairs, weights, weight):
    _, width, rows = halves[0][0].shape
    operands = [*pairs, *weights]
    for own, query_part, two, one, far4, far8 in halves:
        operands += [own, query_part, far4, far8, *two, *one]
    return pl.pallas_call(
        functools.partial(sum_kernel, [(len(h[2]), len(h[3])) for h in halves]),
        in_specs=[VMEM] * len(operands),
        out_specs=pl.BlockSpec(memory_space=pl.ANY),
        out_shape=jax.ShapeDtypeStruct((2 * rows, width), jnp.bfloat16),
        scratch_shapes=[pltpu.VMEM((width, 2 * rows), jnp.bfloat16)] * 2
        + [pltpu.VMEM((2 * rows, width), jnp.bfloat16), pltpu.SemaphoreType.DMA((2,))],
        compiler_params=params(),
        cost_estimate=pl.CostEstimate(flops=int(weight * US_FLOPS), bytes_accessed=int(weight * US), transcendentals=0),
        name="sums",
    )(*operands)


def per_device(queries, keys, values, grad_out, links, w_query, w_key, w_value):
    patches = queries.shape[1]
    half = patches // 2
    head_size = keys.shape[2] // HEADS
    kv0, qg0, owed = pack(queries, keys, values, grad_out, 0, half, True)
    kv1, qg1 = pack(after(queries, kv0), keys, values, grad_out, half, half, False)
    up4_0 = shift(kv0, 4)
    down4_0 = shift(qg0, -4)
    y_a = swap(owed, 2)
    up4_1 = shift(kv1, 4)
    down4_1 = shift(qg1, -4)
    y_b = swap(after(pick((kv1, up4_0), BY_BIT1, 0), y_a, down4_0), 2)
    up8_0 = shift(after(up4_0, down4_0), 4)
    down8_0 = shift(after(down4_0, up4_0), -4)
    c_a = swap(pick((after(kv0, up4_1, down4_1), qg0), BY_BIT0, 2.8), 1)
    y_c = swap(pick((down4_0, up4_1), BY_BIT1, 3), 2)
    up8_1 = shift(after(up4_1, y_b), 4)
    down8_1 = shift(after(down4_1, up8_0, down8_0), -4)
    c_b = swap(pick((kv1, y_b, y_a), (0, 1, 0, 2), 0), 1)
    near0 = products_of(qg0, [kv0, up4_0], (y_a, y_b), (c_a, c_b), 4)
    far0 = products_of(after(qg0, down8_0), [up8_0], (), (), 5.7)
    c_c = swap(after(pick((y_a, y_c, y_b), (0, 1, 1, 2), 0), near0, far0), 1)
    near1 = products_of(qg1, [kv1, up4_1], (y_b, y_c), (c_b, c_c), 0)
    y_d = swap(after(pick((down4_1, qg1), BY_BIT1, 0), up8_0, down8_0), 2)
    far1 = products_of(after(qg1, c_b), [up8_1], (), (), 10)
    pairs = scores_of(links, after(near0, down8_0), near1, far0, far1, head_size, 0)
    self_pair, pair1, pair2, pair4, pair8 = pairs
    came8 = shift(pair8, -8)
    came4 = shift(pair4, -4)
    came2 = shift(pair2, -2)
    came1 = shift(pair1, -1)
    query_part0 = query_part_of(kv0, (y_a, y_b), (c_a, c_b), up4_0, up8_0, pairs, w_query, 0, 0)
    query_part1 = query_part_of(kv1, (y_b, y_c), (c_b, c_c), up4_1, up8_1, pairs, w_query, half, 0)
    c_d = swap(pick((y_d, qg1), BY_BIT0, 0), 1)
    halves = (
        (qg0, query_part0, (y_a, y_c), (c_a, c_c), down4_0, down8_0),
        (qg1, query_part1, (y_d,), (c_d,), down4_1, down8_1),
    )
    out = sums_of(halves, (self_pair, came8, came4, came2, came1), (w_key, w_value), 3)
    return out[None]


def solution(mesh):
    by_frame = P(("dom", "frame"), None, None)
    return jax.shard_map(
        per_device,
        mesh=mesh,
        in_specs=(by_frame,) * 4 + (P(("dom", "frame"), None), P(), P(), P()),
        out_specs=by_frame,
        check_vma=False,
    )
```
